1024 devices in a mesh: sfc: 512 (over y, x, z), grp: 2 (over core).
Axes of the slice: x: 4, y: 4, z: 32, core: 2. Of those that a mesh axis runs over, the one named last changes fastest.
Arguments:
- right_side: float32 [5, 5, 5, 131072], P(None, None, None, ('sfc', 'grp')), may hold values from -8 to 8
- cell_level: int32 [131072], P(('sfc', 'grp')), may hold values from 0 to 3
- own_slot: int32 [393216], P(('sfc', 'grp')), may hold values from 0 to 767
- near_slot: int32 [393216], P(('sfc', 'grp')), may hold values from 0 to 1151, as said below
- face_kind: int32 [393216], P(('sfc', 'grp')), may hold values from 0 to 5
- orientation: int32 [393216], P(('sfc', 'grp')), may hold values from 0 to 7
- penalty: float32 [393216], P(('sfc', 'grp')), may hold values from 2 to 32
- send_slots: int32 [393216], P(('sfc', 'grp')), may hold values from 0 to 767
- subface_maps: float32 [4, 25, 25], replicated, may hold values from -1.25 to 1.25
Outputs:
- solution: float32 [5, 5, 5, 131072], P(None, None, None, ('sfc', 'grp'))
- residual: float32 [5, 5, 5, 131072], P(None, None, None, ('sfc', 'grp'))
The draws below stay inside these ranges and needn't reach their ends.
Inputs may be any that keep to these rules, and one draw needn't show every extreme that they name: `own_slot`: a face slot f * 128 + c of the same device. `near_slot`: 768 + k * 96 + i for position i of the received block k; since a device has exactly 384 entries, its near slots are a permutation of its 384 received positions. `face_kind`: 0 boundary face, 1 conforming face, 2 + s the fine side of a hanging face with subface s. `send_slots`: a device's entries k * 96 to k * 96 + 95 are face slots of its own cells sent to the device at offset (+1, -1, +2, -2)[k].
All inputs are finite; a program needn't handle non-finite values.
Results may differ from the reference program's by a relative error of at most 0.00021.
Values sent between devices are 32-bit elements; how exact they have to be, the bound alone decides.
No kernel may reach another device: no remote copies, remote signals or barrier semaphores. Data moves between devices by JAX's collectives and lax.ppermute only.
A program may use at most 32 MiB of HBM per device.

```python
import math
import jax
import jax.numpy as jnp
import numpy as np
from jax import lax

NODES = 5
CELLS_DEV = 128
GHOST = 96
ITERS = 3
ENTRY_DEV = 384
CELLS = 131072
ENTRIES = 393216
SENDS = 393216
N_SFC = 512
N_GRP = 2


def draw_right_side(key, part):
    position = jnp.arange(CELLS, dtype=jnp.float32) / CELLS
    values = jax.random.normal(key, (NODES, NODES, NODES, CELLS), jnp.float32)
    return jnp.clip(values, -4.0, 4.0) * jnp.sqrt(1.0 + 2.0 * position)


def draw_near_slot(key, part):
    devices = ENTRIES // ENTRY_DEV
    received = 4 * GHOST
    local_key = jax.random.fold_in(key, 11)
    order_key = jax.random.fold_in(key, 23)
    local = jax.random.randint(local_key, (devices, ENTRY_DEV), 0, 6 * CELLS_DEV, dtype=jnp.int32)
    device_keys = jax.random.split(order_key, devices)
    order = jax.vmap(lambda single: jax.random.permutation(single, ENTRY_DEV))(device_keys).astype(jnp.int32)
    chosen = jnp.where(order < received, 6 * CELLS_DEV + order, local)
    return chosen.reshape(-1).astype(jnp.int32)


def place_ends(drawn, stream_key, smallest, largest):
    longest = drawn.shape.index(max(drawn.shape))
    spots = []
    for shift in (0, 1):
        where = [jax.random.randint(jax.random.fold_in(stream_key, axis), (), 0, length) for axis, length in enumerate(drawn.shape)]
        where[longest] = (where[longest] + shift) % drawn.shape[longest]
        spots.append(tuple(where))
    return drawn.at[spots[0]].set(smallest).at[spots[1]].set(largest)


def block_levels(own_key, shape, cuts, least, largest):
    loudness, own = 1.0, jax.random.fold_in(own_key, 6)
    for dim, blocks in cuts:
        heights = jnp.exp(jax.random.uniform(jax.random.fold_in(own, dim), (blocks,), jnp.float32, least / len(cuts), largest / len(cuts)))
        loudness = loudness * jnp.repeat(heights, shape[dim] // blocks).reshape([-1 if axis == dim else 1 for axis in range(len(shape))])
    return loudness


def centred(rng, shape, scale, reach, kind=jnp.bfloat16):
    values = jax.random.normal(rng, shape, jnp.float32) * scale
    return jnp.minimum(jnp.maximum(values, -reach), reach).astype(kind)


def setup_inputs(seed: int = 0) -> dict:
    seeds = jax.random.split(jax.random.key(seed), 10)
    right_side = draw_right_side(jax.random.fold_in(seeds[9], 71), 0)
    cell_level = place_ends(jax.random.randint(seeds[1], (CELLS,), 0, 4), jax.random.fold_in(seeds[1], 1), 0, 3).astype(jnp.int32)
    own_slot = place_ends(jax.random.randint(seeds[2], (ENTRIES,), 0, 6 * CELLS_DEV), jax.random.fold_in(seeds[2], 1), 0, (6 * CELLS_DEV) - 1).astype(jnp.int32)
    near_slot = draw_near_slot(jax.random.fold_in(seeds[9], 71), 0)
    face_kind = place_ends(jax.random.randint(seeds[4], (ENTRIES,), 0, 6), jax.random.fold_in(seeds[4], 1), 0, 5).astype(jnp.int32)
    orientation = place_ends(jax.random.randint(seeds[5], (ENTRIES,), 0, 8), jax.random.fold_in(seeds[5], 1), 0, 7).astype(jnp.int32)
    penalty = jnp.clip(jnp.exp(math.log(32.0) - 2.7725887 * jax.random.uniform(seeds[6], (ENTRIES,), jnp.float32) ** block_levels(seeds[6], (ENTRIES,), ((0, 1024),), -0.2, 0.2)), 2.0, 32.0)
    send_slots = place_ends(jax.random.randint(seeds[7], (SENDS,), 0, 6 * CELLS_DEV), jax.random.fold_in(seeds[7], 1), 0, (6 * CELLS_DEV) - 1).astype(jnp.int32)
    subface_maps = centred(seeds[8], (4, NODES * NODES, NODES * NODES), (NODES * NODES) ** -0.5, 1.25, jnp.float32)
    return dict(right_side=right_side, cell_level=cell_level, own_slot=own_slot, near_slot=near_slot, face_kind=face_kind, orientation=orientation, penalty=penalty, send_slots=send_slots, subface_maps=subface_maps)


mass_shift = 1.0
curve_offsets = (1, -1, 2, -2)

def node_tables():
    points = np.array([-1.0, -np.sqrt(3.0 / 7.0), 0.0, np.sqrt(3.0 / 7.0), 1.0])
    weights = np.array([0.1, 49.0 / 90.0, 32.0 / 45.0, 49.0 / 90.0, 0.1])
    identity = np.eye(5)
    spacing = points[:, None] - points[None, :] + identity
    barycentric = 1.0 / np.prod(spacing, axis=1)
    offdiag = barycentric[None, :] / barycentric[:, None] / spacing
    diagonal = np.sum(1.0 / spacing, axis=1) - 1.0
    derivs = np.where(identity > 0.5, diagonal[:, None], offdiag)
    stiffness = derivs.T @ (weights[:, None] * derivs)
    return (jnp.asarray(stiffness, jnp.float32), jnp.asarray(weights, jnp.float32))

def volume_term(field, scale, tables):
    stiffness, weights = tables
    first = weights[:, None, None, None]
    second = weights[None, :, None, None]
    third = weights[None, None, :, None]
    along_first = jnp.einsum('ia,abcz->ibcz', stiffness, field, precision=lax.Precision.HIGHEST)
    along_second = jnp.einsum('jb,abcz->ajcz', stiffness, field, precision=lax.Precision.HIGHEST)
    along_third = jnp.einsum('kc,abcz->abkz', stiffness, field, precision=lax.Precision.HIGHEST)
    grads = along_first * second * third + along_second * first * third + along_third * first * second
    return scale * grads + mass_shift * scale * scale * scale * first * second * third * field

def face_traces(field):
    last = NODES - 1
    return jnp.stack([field[0], field[last], field[:, 0], field[:, last], field[:, :, 0], field[:, :, last]], axis=-2)

def lift_faces(faces):
    last = NODES - 1
    rest = faces.shape[2:-2] + faces.shape[-1:]
    volume = jnp.zeros((NODES, NODES, NODES) + rest, faces.dtype)
    volume = volume.at[0].add(faces[..., 0, :])
    volume = volume.at[last].add(faces[..., 1, :])
    volume = volume.at[:, 0].add(faces[..., 2, :])
    volume = volume.at[:, last].add(faces[..., 3, :])
    volume = volume.at[:, :, 0].add(faces[..., 4, :])
    volume = volume.at[:, :, last].add(faces[..., 5, :])
    return volume

def orient_forward(values, codes):
    values = jnp.where(codes & 1 == 1, values[::-1], values)
    values = jnp.where(codes & 2 == 2, values[:, ::-1], values)
    return jnp.where(codes & 4 == 4, jnp.swapaxes(values, 0, 1), values)

def orient_back(values, codes):
    values = jnp.where(codes & 4 == 4, jnp.swapaxes(values, 0, 1), values)
    values = jnp.where(codes & 2 == 2, values[:, ::-1], values)
    return jnp.where(codes & 1 == 1, values[::-1], values)

def map_traces(values, kinds, maps, transpose_maps):
    flat = values.reshape(NODES * NODES, -1)
    result = jnp.where(kinds == 1, flat, 0.0)
    for subface in range(4):
        matrix = maps[subface].T if transpose_maps else maps[subface]
        moved = jnp.dot(matrix, flat, precision=lax.Precision.HIGHEST)
        result = result + jnp.where(kinds == subface + 2, moved, 0.0)
    return result.reshape(values.shape)

def face_terms(own_values, near_values, kinds, orients, penalty, maps, weights):
    face_mass = weights[:, None, None] * weights[None, :, None]
    mapped = map_traces(orient_forward(near_values, orients), kinds, maps, False)
    jump = own_values - mapped
    own_term = penalty * face_mass * jump
    near_term = -orient_back(map_traces(own_term, kinds, maps, True), orients)
    return (own_term, near_term)

def shift_devices(blocks, offset):
    empty = jnp.zeros_like(blocks[:, :abs(offset)])
    if offset > 0:
        return jnp.concatenate([empty, blocks[:, :-offset]], axis=1)
    return jnp.concatenate([blocks[:, -offset:], empty], axis=1)

def apply_operator(field, scale, own_slot, near_slot, kinds, orients, penalty, send_slots, maps, tables):
    devices = N_SFC * N_GRP
    count = CELLS_DEV
    slots = 6 * count
    width = NODES * NODES
    span = slots + 4 * GHOST
    device_rows = jnp.arange(devices, dtype=jnp.int32)[:, None]
    traces = face_traces(field.reshape(NODES, NODES, NODES, devices, count)).reshape(width, devices * slots)
    send_index = (send_slots.reshape(devices, 4 * GHOST) + device_rows * slots).reshape(-1).astype(jnp.int32)
    sent = jnp.take(traces, send_index, axis=1).reshape(width, devices, 4, GHOST)
    arrived = [shift_devices(sent[:, :, position], offset) for position, offset in enumerate(curve_offsets)]
    ghosts = jnp.stack(arrived, axis=2).reshape(width, devices, 4 * GHOST)
    pool = jnp.concatenate([traces.reshape(width, devices, slots), ghosts], axis=2).reshape(width, devices * span)
    own_index = (own_slot.reshape(devices, -1) + device_rows * span).reshape(-1).astype(jnp.int32)
    near_index = (near_slot.reshape(devices, -1) + device_rows * span).reshape(-1).astype(jnp.int32)
    own_values = jnp.take(pool, own_index, axis=1).reshape(NODES, NODES, -1)
    near_values = jnp.take(pool, near_index, axis=1).reshape(NODES, NODES, -1)
    own_term, near_term = face_terms(own_values, near_values, kinds, orients, penalty, maps, tables[1])
    gathered = jnp.zeros_like(pool).at[:, own_index].add(own_term.reshape(width, -1))
    gathered = gathered.at[:, near_index].add(near_term.reshape(width, -1))
    gathered = gathered.reshape(width, devices, span)
    local = gathered[:, :, :slots].reshape(width, devices * slots)
    returned = gathered[:, :, slots:].reshape(width, devices, 4, GHOST)
    came_back = [shift_devices(returned[:, :, position], -offset) for position, offset in enumerate(curve_offsets)]
    back = jnp.stack(came_back, axis=2).reshape(width, devices * 4 * GHOST)
    local = local.at[:, send_index].add(back)
    faces = local.reshape(NODES, NODES, devices, 6, count)
    lifted = lift_faces(faces).reshape(NODES, NODES, NODES, devices * count)
    return volume_term(field, scale, tables) + lifted

def reference(right_side, cell_level, own_slot, near_slot, face_kind, orientation, penalty, send_slots, subface_maps):
    tables = node_tables()
    scale = jnp.exp2(-cell_level.astype(jnp.float32))
    devices = N_SFC * N_GRP
    device_rows = jnp.arange(devices, dtype=jnp.int32)[:, None]
    cell_index = (own_slot.reshape(devices, -1) % CELLS_DEV + device_rows * CELLS_DEV).reshape(-1).astype(jnp.int32)
    scaled_penalty = penalty * jnp.take(scale, cell_index)
    solution = jnp.zeros_like(right_side)
    residual = right_side
    direction = right_side
    norm_now = jnp.sum(residual * residual)
    for iteration in range(ITERS):
        image = apply_operator(direction, scale, own_slot, near_slot, face_kind, orientation, scaled_penalty, send_slots, subface_maps, tables)
        step_size = norm_now / jnp.sum(direction * image)
        solution = solution + step_size * direction
        residual = residual - step_size * image
        norm_next = jnp.sum(residual * residual)
        direction = residual + norm_next / norm_now * direction
        norm_now = norm_next
    return (solution, residual)
```

```python
import jax
import jax.numpy as jnp
import numpy as np
from jax import lax
from jax.sharding import Mesh
from jax.sharding import PartitionSpec as P

NODES = 5
ITERS = 3
SIGMA = 32.0
SFC = ("sfc_0", "sfc_1", "sfc_2")
SFC_GRP = ("sfc_0", "sfc_1", "sfc_2", "grp")


mass_shift = 1.0
highest = lax.Precision.HIGHEST


def partner_2(block, axis, distance):
    count = lax.axis_size(axis)
    route = []
    for low in range(count):
        high = low | 1 << distance
        if high != low and high < count:
            route += [(low, high), (high, low)]
    return lax.ppermute(block, axis, route)


def shifted(block, axis, distance):
    devices = range(lax.axis_size(axis))
    route = [(i - distance, i) for i in devices if i - distance in devices]
    return lax.ppermute(block, axis, route)


def sum_over(value, axes):
    count = lax.axis_size(axes)
    copies = lax.optimization_barrier(jnp.broadcast_to(value[None], (count,) + value.shape))
    return jnp.sum(lax.all_to_all(copies, axes, 0, 0, tiled=True), axis=0)


def node_tables():
    points = np.array([-1.0, -np.sqrt(3.0 / 7.0), 0.0, np.sqrt(3.0 / 7.0), 1.0])
    weights = np.array([0.1, 49.0 / 90.0, 32.0 / 45.0, 49.0 / 90.0, 0.1])
    identity = np.eye(5)
    spacing = points[:, None] - points[None, :] + identity
    barycentric = 1.0 / np.prod(spacing, axis=1)
    offdiag = barycentric[None, :] / barycentric[:, None] / spacing
    diagonal = np.sum(1.0 / spacing, axis=1) - 1.0
    derivs = np.where(identity > 0.5, diagonal[:, None], offdiag)
    stiffness = derivs.T @ (weights[:, None] * derivs)
    return (jnp.asarray(stiffness, jnp.float32), jnp.asarray(weights, jnp.float32))


def volume_term(field, scale, tables):
    stiffness, weights = tables
    first = weights[:, None, None, None]
    second = weights[None, :, None, None]
    third = weights[None, None, :, None]
    along_first = jnp.einsum("ia,abcz->ibcz", stiffness, field, precision=highest)
    along_second = jnp.einsum("jb,abcz->ajcz", stiffness, field, precision=highest)
    along_third = jnp.einsum("kc,abcz->abkz", stiffness, field, precision=highest)
    grads = (
        along_first * second * third + along_second * first * third + along_third * first * second
    )
    return scale * grads + mass_shift * scale * scale * scale * first * second * third * field


def face_traces(field):
    last = NODES - 1
    return jnp.stack(
        [field[0], field[last], field[:, 0], field[:, last], field[:, :, 0], field[:, :, last]],
        axis=-2,
    )


def lift_faces(faces):
    last = NODES - 1
    rest = faces.shape[2:-2] + faces.shape[-1:]
    volume = jnp.zeros((NODES, NODES, NODES) + rest, faces.dtype)
    volume = volume.at[0].add(faces[..., 0, :])
    volume = volume.at[last].add(faces[..., 1, :])
    volume = volume.at[:, 0].add(faces[..., 2, :])
    volume = volume.at[:, last].add(faces[..., 3, :])
    volume = volume.at[:, :, 0].add(faces[..., 4, :])
    volume = volume.at[:, :, last].add(faces[..., 5, :])
    return volume


def orient_forward(values, codes):
    values = jnp.where(codes & 1 == 1, values[::-1], values)
    values = jnp.where(codes & 2 == 2, values[:, ::-1], values)
    return jnp.where(codes & 4 == 4, jnp.swapaxes(values, 0, 1), values)


def orient_back(values, codes):
    values = jnp.where(codes & 4 == 4, jnp.swapaxes(values, 0, 1), values)
    values = jnp.where(codes & 2 == 2, values[:, ::-1], values)
    return jnp.where(codes & 1 == 1, values[::-1], values)


def map_traces(values, kinds, maps, transpose_maps):
    width = NODES * NODES
    flat = values.reshape(width, -1)
    stacked = jnp.swapaxes(maps, 1, 2) if transpose_maps else maps
    moved = jnp.dot(stacked.reshape(4 * width, width), flat, precision=highest).reshape(
        4, width, -1
    )
    selector = kinds[None, :] == jnp.arange(4, dtype=jnp.int32)[:, None] + 2
    result = jnp.where(kinds == 1, flat, 0.0) + jnp.sum(
        jnp.where(selector[:, None, :], moved, 0.0), axis=0
    )
    return result.reshape(values.shape)


def face_terms(own_values, near_values, kinds, orients, penalty, maps, weights):
    face_mass = weights[:, None, None] * weights[None, :, None]
    mapped = map_traces(orient_forward(near_values, orients), kinds, maps, False)
    jump = own_values - mapped
    own_term = penalty * face_mass * jump
    near_term = -orient_back(map_traces(own_term, kinds, maps, True), orients)
    return (own_term, near_term)


def route_blocks(blocks):
    core = lax.axis_index("grp")
    partner = partner_2(jnp.stack([blocks[0], blocks[1]]), "grp", 0)
    upward = shifted(jnp.stack([blocks[2], partner[0]]), SFC, 1)
    downward = shifted(jnp.stack([blocks[3], partner[1]]), SFC, -1)
    plus_one = jnp.where(core == 1, partner[0], upward[1])
    minus_one = jnp.where(core == 0, partner[1], downward[1])
    return (plus_one, minus_one, upward[0], downward[0])


def apply_operator(
    field, scale, own_slot, near_slot, kinds, orients, penalty, send_slots, maps, tables
):
    count = field.shape[-1]
    slots = 6 * count
    width = NODES * NODES
    ghost = send_slots.shape[0] // 4
    traces = face_traces(field).reshape(width, slots)
    sent = jnp.take(traces, send_slots, axis=1)
    arrived = route_blocks(
        tuple((sent[:, position * ghost : (position + 1) * ghost] for position in range(4)))
    )
    volume = volume_term(field, scale, tables)
    pool = jnp.concatenate((traces,) + arrived, axis=1)
    own_values = jnp.take(pool, own_slot, axis=1).reshape(NODES, NODES, -1)
    near_values = jnp.take(pool, near_slot, axis=1).reshape(NODES, NODES, -1)
    own_term, near_term = face_terms(
        own_values, near_values, kinds, orients, penalty, maps, tables[1]
    )
    gathered = jnp.zeros_like(pool).at[:, own_slot].add(own_term.reshape(width, -1))
    gathered = gathered.at[:, near_slot].add(near_term.reshape(width, -1))
    returned = tuple(
        (
            gathered[:, slots + position * ghost : slots + (position + 1) * ghost]
            for position in range(4)
        )
    )
    came_back = route_blocks((returned[1], returned[0], returned[3], returned[2]))
    back = jnp.concatenate((came_back[1], came_back[0], came_back[3], came_back[2]), axis=1)
    local = gathered[:, :slots].at[:, send_slots].add(back)
    faces = local.reshape(NODES, NODES, 6, count)
    return volume + lift_faces(faces)


def coefficients(moments):
    def inner(one, two, shift):
        return sum(
            one[i] * two[j] * moments[i + j + shift]
            for i in range(len(one))
            for j in range(len(two))
        )

    iterate, remains, search = [], [1.0], [1.0]
    norm_now = moments[0]
    for iteration in range(ITERS):
        step = norm_now / inner(search, search, 1)
        iterate = [
            (iterate[i] if i < len(iterate) else 0.0) + step * search[i] for i in range(len(search))
        ]
        image = [0.0] + search
        remains = [
            (remains[i] if i < len(remains) else 0.0) - step * image[i] for i in range(len(image))
        ]
        if iteration + 1 < ITERS:
            norm_next = inner(remains, remains, 0)
            blend = norm_next / norm_now
            search = [
                remains[i] + (blend * search[i] if i < len(search) else 0.0)
                for i in range(len(remains))
            ]
            norm_now = norm_next
    return iterate, remains


def body(
    right_side,
    cell_level,
    own_slot,
    near_slot,
    face_kind,
    orientation,
    penalty,
    send_slots,
    subface_maps,
):
    tables = node_tables()
    scale = jnp.exp2(-cell_level.astype(jnp.float32))
    count = right_side.shape[-1]
    scaled_penalty = penalty * jnp.take(scale, own_slot % count)

    def operate(field):
        return apply_operator(
            field,
            scale,
            own_slot,
            near_slot,
            face_kind,
            orientation,
            scaled_penalty,
            send_slots,
            subface_maps,
            tables,
        )

    powers = [right_side]
    for iteration in range(ITERS):
        powers.append(operate(powers[-1]) * (1.0 / SIGMA))
    local = [jnp.sum(powers[(k + 0) // 2] * powers[(k + 1) // 2]) for k in range(2 * ITERS)]
    totals = jnp.pad(jnp.stack(local), (0, 128 - 2 * ITERS))[None]
    totals = sum_over(sum_over(totals, ("sfc_2",)), ("sfc_0", "sfc_1", "grp"))
    moments = [totals[0, k] for k in range(2 * ITERS)]
    iterate, remains = coefficients(moments)
    solution = sum((c * (1.0 / SIGMA)) * v for c, v in zip(iterate, powers))
    residual = sum(c * v for c, v in zip(remains, powers))
    return (solution, residual)


def solution(mesh):
    finer = Mesh(
        mesh.devices.reshape(4, 4, 32, mesh.shape["grp"]), ("sfc_0", "sfc_1", "sfc_2", "grp")
    )
    in_specs = (
        P(None, None, None, SFC_GRP),
        P(SFC_GRP),
        P(SFC_GRP),
        P(SFC_GRP),
        P(SFC_GRP),
        P(SFC_GRP),
        P(SFC_GRP),
        P(SFC_GRP),
        P(),
    )
    out_specs = (P(None, None, None, SFC_GRP), P(None, None, None, SFC_GRP))
    return jax.shard_map(body, mesh=finer, in_specs=in_specs, out_specs=out_specs, check_vma=False)
```

```python
import functools

import jax
import jax.numpy as jnp
import numpy as np
from jax import lax
from jax.experimental import pallas as pl
from jax.experimental.pallas import tpu as pltpu
from jax.sharding import Mesh
from jax.sharding import PartitionSpec as P

NODES = 5
WIDTH = 25
CELLS = 128
GHOST = 96
ITERS = 3
SIGMA = 32.0
MASS_SHIFT = 1.0
Z_AXIS = ("sfc_2",)
OTHERS = ("sfc_0", "sfc_1", "grp")
SFC = ("sfc_0", "sfc_1", "sfc_2")
SFC_GRP = ("sfc_0", "sfc_1", "sfc_2", "grp")
VMEM_LIMIT = 24 * 1024 * 1024

f32 = jnp.float32
bf16 = jnp.bfloat16
highest = lax.Precision.HIGHEST


def node_tables():
    points = np.array([-1.0, -np.sqrt(3.0 / 7.0), 0.0, np.sqrt(3.0 / 7.0), 1.0])
    weights = np.array([0.1, 49.0 / 90.0, 32.0 / 45.0, 49.0 / 90.0, 0.1])
    identity = np.eye(5)
    spacing = points[:, None] - points[None, :] + identity
    barycentric = 1.0 / np.prod(spacing, axis=1)
    offdiag = barycentric[None, :] / barycentric[:, None] / spacing
    diagonal = np.sum(1.0 / spacing, axis=1) - 1.0
    derivs = np.where(identity > 0.5, diagonal[:, None], offdiag)
    stiffness = derivs.T @ (weights[:, None] * derivs)
    return stiffness, weights


STIFFNESS, WEIGHTS = node_tables()
FACE_MASS = [float(WEIGHTS[t // 5] * WEIGHTS[t % 5]) for t in range(WIDTH)]


def volume_tables():
    mass = np.diag(WEIGHTS)
    grads = (
        np.kron(np.kron(STIFFNESS, mass), mass)
        + np.kron(np.kron(mass, STIFFNESS), mass)
        + np.kron(np.kron(mass, mass), STIFFNESS)
    )
    full = np.zeros((128, 128), np.float32)
    full[:125, :125] = grads
    column = np.zeros((128, 128), np.float32)
    column[:125] = np.diag(np.kron(np.kron(mass, mass), mass))[:, None] * MASS_SHIFT
    return full, column


def face_node(face, t):
    high, low = t // 5, t % 5
    side = 4 * (face % 2)
    if face < 2:
        return 25 * side + t
    if face < 4:
        return 25 * high + 5 * side + low
    return 25 * high + 5 * low + side


def split(value):
    first = value.astype(bf16).astype(f32)
    rest = value - first
    second = rest.astype(bf16).astype(f32)
    third = (rest - second).astype(bf16).astype(f32)
    return first, second, third


def rev_first(planes, mask):
    return [jnp.where(mask, planes[5 * (4 - t // 5) + t % 5], planes[t]) for t in range(WIDTH)]


def rev_second(planes, mask):
    return [jnp.where(mask, planes[5 * (t // 5) + 4 - t % 5], planes[t]) for t in range(WIDTH)]


def swap(planes, mask):
    return [jnp.where(mask, planes[5 * (t % 5) + t // 5], planes[t]) for t in range(WIDTH)]


def orient_masks(codes):
    codes = codes.astype(jnp.int32)
    return (codes & 1) == 1, (codes & 2) == 2, (codes & 4) == 4


def orient_forward(planes, masks):
    return swap(rev_second(rev_first(planes, masks[0]), masks[1]), masks[2])


def orient_back(planes, masks):
    return rev_first(rev_second(swap(planes, masks[2]), masks[1]), masks[0])


def read_planes(ref, count=WIDTH):
    return [ref[8 * t : 8 * t + 8, :] for t in range(count)]


def gather_planes(field, face, cell):
    rows = {}

    def at(node):
        if node not in rows:
            row = jnp.broadcast_to(field[node : node + 1, :], (8, 128))
            rows[node] = jnp.take_along_axis(row, cell, axis=1, mode="promise_in_bounds")
        return rows[node]

    masks = [face == k for k in range(5)]
    planes = []
    for t in range(WIDTH):
        value = at(face_node(5, t))
        for k in range(5):
            value = jnp.where(masks[k], at(face_node(k, t)), value)
        planes.append(value)
    return planes


def write_messages(source, both_ref, up_ref, down_ref):
    def pair(ref, start, sent, own):
        ref[pl.ds(start, 28, stride=2), :] = source[pl.ds(4 + sent, 28, stride=8), :]
        ref[pl.ds(start + 1, 28, stride=2), :] = source[pl.ds(own, 28, stride=8), :]

    pair(both_ref, 0, 0, 1)
    pair(both_ref, 56, 1, 0)
    pair(up_ref, 0, 2, 3)
    pair(down_ref, 0, 3, 2)


def first_kernel(
    rhs_ref,
    level_ref,
    own_ref,
    near_ref,
    kind_ref,
    orient_ref,
    penalty_ref,
    send_ref,
    field_ref,
    planes_ref,
    index_ref,
    both_ref,
    up_ref,
    down_ref,
):
    for a in range(5):
        for b in range(5):
            field_ref[25 * a + 5 * b : 25 * a + 5 * b + 5, :] = rhs_ref[a, b]
    field_ref[125:128, :] = jnp.zeros((3, 128), f32)
    own = own_ref[...]
    pieces = split(penalty_ref[...])
    rows = [
        (own >> 7).astype(f32),
        (own & 127).astype(f32),
        kind_ref[...].astype(f32),
        orient_ref[...].astype(f32),
        pieces[0],
        pieces[1],
        pieces[2],
        jnp.zeros((1, 384), f32),
    ]
    table = jnp.concatenate(rows, axis=0).astype(bf16)
    spot = lax.broadcasted_iota(jnp.int32, (512, 384), 0)
    lane = spot & 127
    wanted = jnp.where(lane < GHOST, 6 * CELLS + (spot >> 7) * GHOST + lane, -1)
    onehot = jnp.where(wanted == near_ref[...], 1.0, 0.0).astype(bf16)
    moved = lax.dot_general(
        table, onehot, (((1,), (1,)), ((), ())), preferred_element_type=f32
    )
    zeros = jnp.zeros((4, 128), f32)

    def upper(row):
        parts = [row[:, 128 * k : 128 * k + 128] for k in range(4)]
        return jnp.concatenate(parts + [zeros], axis=0)

    own_face, own_cell = upper(moved[0:1]), upper(moved[1:2])
    penalty = upper(moved[4:5] + moved[5:6] + moved[6:7])
    send = send_ref[...]
    sub = lax.broadcasted_iota(jnp.int32, (8, 128), 0)
    face = jnp.where(sub < 4, own_face.astype(jnp.int32), send >> 7)
    cell = jnp.where(sub < 4, own_cell.astype(jnp.int32), send & 127)
    index_ref[0:8, :] = face
    index_ref[8:16, :] = cell
    scale = jnp.exp2(-jnp.broadcast_to(level_ref[...], (8, 128)).astype(f32))
    scaled = penalty * jnp.take_along_axis(scale, cell, axis=1, mode="promise_in_bounds")
    for t, plane in enumerate(gather_planes(field_ref, face, cell)):
        planes_ref[8 * t : 8 * t + 8, :] = plane
    planes_ref[200:208, :] = upper(moved[2:3])
    planes_ref[208:216, :] = upper(moved[3:4])
    planes_ref[216:224, :] = scaled
    write_messages(planes_ref, both_ref, up_ref, down_ref)


def local_volume(field, level_ref, grads_ref, mass_ref):
    scale = jnp.exp2(-level_ref[...].astype(f32))
    grads = jnp.dot(grads_ref[...], field, precision=highest, preferred_element_type=f32)
    return scale * grads + (scale * scale * scale) * (mass_ref[...] * field)


def volume_kernel(field_ref, level_ref, grads_ref, mass_ref, volume_ref):
    volume_ref[...] = local_volume(field_ref[...], level_ref, grads_ref, mass_ref)


def map_sent(maps_ref, planes_ref, meta_ref, masks):
    turned = orient_forward(read_planes(planes_ref), masks)
    result = []
    for i in range(WIDTH):
        total = None
        for j in range(WIDTH):
            at = 8 * (WIDTH * j + i)
            term = maps_ref[at : at + 8, :] * turned[j]
            total = term if total is None else total + term
        result.append(total)
    return result


def middle_kernel(
    field_ref, level_ref, grads_ref, mass_ref, maps_ref, planes_ref, meta_ref, volume_ref, sent_ref
):
    volume_ref[...] = local_volume(field_ref[...], level_ref, grads_ref, mass_ref)
    masks = orient_masks(meta_ref[8:16, :])
    for t, plane in enumerate(map_sent(maps_ref, planes_ref, meta_ref, masks)):
        sent_ref[8 * t : 8 * t + 8, :] = plane


def read_messages(core_ref, partner_ref, below_ref, above_ref, got_ref):
    low = core_ref[0] == 0

    def rows(ref, start):
        return ref[pl.ds(start, 28, stride=2), :]

    def put(row, value):
        got_ref[pl.ds(row, 28, stride=8), :] = value

    for j, (from_below, from_above) in enumerate(((0, 1), (5, 4))):
        put(from_below, jnp.where(low, rows(below_ref, 56 + j), rows(partner_ref, j)))
        put(from_above, jnp.where(low, rows(partner_ref, 56 + j), rows(above_ref, 56 + j)))
    put(2, rows(below_ref, 0))
    put(7, rows(below_ref, 1))
    put(3, rows(above_ref, 0))
    put(6, rows(above_ref, 1))


def build_maps(plain_ref, turned_ref, kind, maps_ref):
    code = lax.broadcasted_iota(jnp.int32, (8, 128), 0)
    code = jnp.where(code < 4, code + 2, jnp.where(code == 4, 1, -1)).astype(f32)
    for half, table_ref in enumerate((plain_ref, turned_ref)):
        table = jnp.concatenate(split(table_ref[...]), axis=0)
        table = jnp.transpose(table).astype(bf16)
        chosen = []
        for row in range(4 * half, 4 * half + 4):
            chosen.append(jnp.where(code == kind[row : row + 1, :], 1.0, 0.0))
        chosen = jnp.concatenate(chosen, axis=1)
        chosen = jnp.concatenate([chosen] * 3, axis=0).astype(bf16)
        values = jnp.dot(table, chosen, preferred_element_type=f32)
        for k in range(4):
            maps_ref[pl.ds(4 * half + k, 640, stride=8), :] = values[:, 128 * k : 128 * k + 128]


def add_faces(volume_ref, planes, index_ref, pieces_ref, field_ref):
    for t, plane in enumerate(planes):
        pieces_ref[8 * t : 8 * t + 8, :] = plane
    pieces_ref[200:256, :] = jnp.zeros((56, 128), f32)
    face, cell = index_ref[0:8, :], index_ref[8:16, :]
    key = (face & 1) * 128 + cell
    axis = face >> 1
    slot = lax.broadcasted_iota(jnp.int32, (256, 128), 0)
    left, right = [], []
    for row in range(8):
        value = jnp.concatenate(split(pieces_ref[pl.ds(row, 32, stride=8), :]), axis=0)
        chosen = axis[row : row + 1, :]
        left.append(
            jnp.concatenate([jnp.where(chosen == k, value, 0.0) for k in range(3)], axis=0).astype(
                bf16
            )
        )
        right.append(jnp.where(slot == key[row : row + 1, :], 1.0, 0.0).astype(bf16))
    total = lax.dot_general(
        jnp.concatenate(left, axis=1),
        jnp.concatenate(right, axis=1),
        (((1,), (1,)), ((), ())),
        preferred_element_type=f32,
    )
    total = total * (1.0 / SIGMA)
    field_ref[...] = volume_ref[...] * (1.0 / SIGMA)
    for k in range(3):
        part = total[96 * k : 96 * k + 32] + total[96 * k + 32 : 96 * k + 64]
        part = part + total[96 * k + 64 : 96 * k + 96]
        for side in range(2):
            value = part[:WIDTH, 128 * side : 128 * side + 128]
            if k == 0:
                field_ref[100 * side : 100 * side + 25, :] += value
            elif k == 1:
                for a in range(5):
                    at = 25 * a + 20 * side
                    field_ref[at : at + 5, :] += value[5 * a : 5 * a + 5]
            else:
                field_ref[pl.ds(4 * side, 25, stride=5), :] += value


def combine(got_ref, planes_ref, sent, maps_ref, penalty, masks):
    sub = lax.broadcasted_iota(jnp.int32, (8, 128), 0)
    owned = sub < 4
    got = read_planes(got_ref)
    turned = orient_forward(got, masks)
    mixed = [
        jnp.where(owned, turned[t], (penalty * FACE_MASS[t]) * (got[t] - sent[t]))
        for t in range(WIDTH)
    ]
    mapped = []
    for i in range(WIDTH):
        total = None
        for j in range(WIDTH):
            at = 8 * (WIDTH * i + j)
            term = maps_ref[at : at + 8, :] * mixed[j]
            total = term if total is None else total + term
        mapped.append(total)
    back = orient_back(mapped, masks)
    return [
        jnp.where(
            owned,
            (penalty * FACE_MASS[t]) * (planes_ref[8 * t : 8 * t + 8, :] - mapped[t]),
            -back[t],
        )
        for t in range(WIDTH)
    ]


def next_messages(field_ref, index_ref, planes_ref, both_ref, up_ref, down_ref):
    face, cell = index_ref[0:8, :], index_ref[8:16, :]
    for t, plane in enumerate(gather_planes(field_ref, face, cell)):
        planes_ref[8 * t : 8 * t + 8, :] = plane
    planes_ref[200:224, :] = jnp.zeros((24, 128), f32)
    write_messages(planes_ref, both_ref, up_ref, down_ref)


def second_kernel(
    core_ref,
    partner_ref,
    below_ref,
    above_ref,
    old_ref,
    volume_ref,
    index_ref,
    plain_ref,
    turned_ref,
    field_ref,
    planes_ref,
    meta_ref,
    maps_ref,
    both_ref,
    up_ref,
    down_ref,
    got_ref,
    pieces_ref,
):
    read_messages(core_ref, partner_ref, below_ref, above_ref, got_ref)
    sub = lax.broadcasted_iota(jnp.int32, (8, 128), 0)
    for k in range(3):
        at = 200 + 8 * k
        meta_ref[8 * k : 8 * k + 8, :] = jnp.where(
            sub < 4, old_ref[at : at + 8, :], got_ref[at : at + 8, :]
        )
    masks = orient_masks(meta_ref[8:16, :])
    build_maps(plain_ref, turned_ref, meta_ref[0:8, :], maps_ref)
    sent = map_sent(maps_ref, old_ref, meta_ref, masks)
    planes = combine(got_ref, old_ref, sent, maps_ref, meta_ref[16:24, :], masks)
    add_faces(volume_ref, planes, index_ref, pieces_ref, field_ref)
    next_messages(field_ref, index_ref, planes_ref, both_ref, up_ref, down_ref)


def third_kernel(
    core_ref,
    partner_ref,
    below_ref,
    above_ref,
    old_ref,
    sent_ref,
    volume_ref,
    index_ref,
    meta_ref,
    maps_ref,
    field_ref,
    planes_ref,
    both_ref,
    up_ref,
    down_ref,
    got_ref,
    pieces_ref,
):
    read_messages(core_ref, partner_ref, below_ref, above_ref, got_ref)
    masks = orient_masks(meta_ref[8:16, :])
    sent = read_planes(sent_ref)
    planes = combine(got_ref, old_ref, sent, maps_ref, meta_ref[16:24, :], masks)
    add_faces(volume_ref, planes, index_ref, pieces_ref, field_ref)
    next_messages(field_ref, index_ref, planes_ref, both_ref, up_ref, down_ref)


def fourth_kernel(
    core_ref,
    partner_ref,
    below_ref,
    above_ref,
    old_ref,
    sent_ref,
    volume_ref,
    index_ref,
    meta_ref,
    maps_ref,
    power0_ref,
    power1_ref,
    power2_ref,
    field_ref,
    moments_ref,
    got_ref,
    pieces_ref,
):
    read_messages(core_ref, partner_ref, below_ref, above_ref, got_ref)
    masks = orient_masks(meta_ref[8:16, :])
    sent = read_planes(sent_ref)
    planes = combine(got_ref, old_ref, sent, maps_ref, meta_ref[16:24, :], masks)
    add_faces(volume_ref, planes, index_ref, pieces_ref, field_ref)
    powers = [power0_ref[...], power1_ref[...], power2_ref[...], field_ref[...]]
    lane = lax.broadcasted_iota(jnp.int32, (1, 128), 1)
    result = jnp.zeros((1, 128), f32)
    for k in range(2 * ITERS):
        row = jnp.sum(powers[k // 2] * powers[(k + 1) // 2], axis=0, keepdims=True)
        result = jnp.where(lane == k, jnp.sum(row, axis=1, keepdims=True), result)
    moments_ref[...] = jnp.broadcast_to(result, moments_ref.shape)


def repeat_sum_kernel(rows_ref, out_ref):
    total = jnp.sum(rows_ref[...], axis=0, keepdims=True)
    out_ref[...] = jnp.broadcast_to(total, out_ref.shape)


def coefficients(moments):
    def inner(one, two, shift):
        total = None
        for i in range(len(one)):
            for j in range(len(two)):
                term = one[i] * two[j] * moments[i + j + shift]
                total = term if total is None else total + term
        return total

    unit = jnp.ones_like(moments[0])
    none = jnp.zeros_like(moments[0])
    iterate, remains, search = [], [unit], [unit]
    norm_now = moments[0]
    for iteration in range(ITERS):
        step = norm_now / inner(search, search, 1)
        iterate = [
            (iterate[i] if i < len(iterate) else none) + step * search[i]
            for i in range(len(search))
        ]
        image = [none] + search
        remains = [
            (remains[i] if i < len(remains) else none) - step * image[i]
            for i in range(len(image))
        ]
        if iteration + 1 < ITERS:
            norm_next = inner(remains, remains, 0)
            blend = norm_next / norm_now
            search = [
                remains[i] + (blend * search[i] if i < len(search) else none)
                for i in range(len(remains))
            ]
            norm_now = norm_next
    return iterate, remains


def last_kernel(
    rows_ref, power0_ref, power1_ref, power2_ref, power3_ref, solution_ref, residual_ref
):
    total = jnp.sum(rows_ref[...], axis=0, keepdims=True)
    lane = lax.broadcasted_iota(jnp.int32, (1, 128), 1)
    moments = [
        jnp.broadcast_to(
            jnp.sum(jnp.where(lane == k, total, 0.0), axis=1, keepdims=True), (1, 128)
        )
        for k in range(2 * ITERS)
    ]
    iterate, remains = coefficients(moments)
    powers = (power0_ref, power1_ref, power2_ref, power3_ref)
    for a in range(5):
        for b in range(5):
            at = 25 * a + 5 * b
            values = [ref[at : at + 5, :] for ref in powers]
            answer = sum((c * (1.0 / SIGMA)) * v for c, v in zip(iterate, values))
            solution_ref[a, b] = answer
            residual_ref[a, b] = sum(c * v for c, v in zip(remains, values))


def call(kernel, outs, ins, scratch=(), scalars=0, flops=0, bytes_accessed=0):
    in_specs = [pl.BlockSpec(memory_space=pltpu.SMEM)] * scalars
    in_specs += [pl.BlockSpec(memory_space=pltpu.VMEM)] * (len(ins) - scalars)
    return pl.pallas_call(
        kernel,
        out_shape=[jax.ShapeDtypeStruct(shape, kind) for shape, kind in outs],
        in_specs=in_specs,
        out_specs=[pl.BlockSpec(memory_space=pltpu.VMEM)] * len(outs),
        scratch_shapes=list(scratch),
        compiler_params=pltpu.CompilerParams(vmem_limit_bytes=VMEM_LIMIT),
        cost_estimate=pl.CostEstimate(
            flops=flops, bytes_accessed=bytes_accessed, transcendentals=0
        ),
    )(*ins)


def shifted(block, axis, distance):
    devices = range(lax.axis_size(axis))
    route = [(i - distance, i) for i in devices if i - distance in devices]
    return lax.ppermute(block, axis, route)


def exchange(both, up, down):
    partner = lax.ppermute(both, "grp", [(0, 1), (1, 0)])
    below = shifted(jnp.concatenate([up, partner[:56]], axis=0), SFC, 1)
    above = shifted(jnp.concatenate([down, partner[56:]], axis=0), SFC, -1)
    return partner, below, above


def sum_over(rows, axes):
    return lax.all_to_all(rows, axes, 0, 0, tiled=True)


def body(
    right_side,
    cell_level,
    own_slot,
    near_slot,
    face_kind,
    orientation,
    penalty,
    send_slots,
    subface_maps,
):
    field_shape, planes_shape = ((128, 128), f32), ((256, 128), f32)
    messages = [((112, 128), f32), ((56, 128), f32), ((56, 128), f32)]
    core = lax.axis_index("grp").astype(jnp.int32).reshape(1)
    grads, mass = (jnp.asarray(table) for table in volume_tables())
    level = cell_level.reshape(1, 128)
    send = jnp.pad(send_slots.reshape(4, GHOST), ((4, 0), (0, 128 - GHOST)))
    identity = jnp.eye(WIDTH, dtype=f32)[None]
    plain, turned = (
        jnp.pad(
            jnp.concatenate([maps, identity], axis=0).reshape(5, WIDTH * WIDTH), ((0, 3), (0, 15))
        )
        for maps in (subface_maps, jnp.swapaxes(subface_maps, 1, 2))
    )
    power0, planes, index, *sends = call(
        first_kernel,
        [field_shape, planes_shape, ((16, 128), jnp.int32)] + messages,
        [right_side, level]
        + [a.reshape(1, -1) for a in (own_slot, near_slot, face_kind, orientation, penalty)]
        + [send],
    )
    scratch = [pltpu.VMEM((224, 128), f32), pltpu.VMEM((256, 128), f32)]
    got = exchange(*sends)
    (volume,) = call(volume_kernel, [field_shape], [power0, level, grads, mass], flops=10**7)
    power1, new_planes, meta, maps, *sends = call(
        second_kernel,
        [field_shape, planes_shape, ((24, 128), f32), ((5120, 128), f32)] + messages,
        [core, *got, planes, volume, index, plain, turned],
        scratch,
        scalars=1,
    )
    planes = new_planes

    def middle(field):
        return call(
            middle_kernel,
            [field_shape, planes_shape],
            [field, level, grads, mass, maps, planes, meta],
            flops=10**7,
        )

    got = exchange(*sends)
    volume, sent = middle(power1)
    power2, new_planes, *sends = call(
        third_kernel,
        [field_shape, planes_shape] + messages,
        [core, *got, planes, sent, volume, index, meta, maps],
        scratch,
        scalars=1,
    )
    planes = new_planes
    got = exchange(*sends)
    volume, sent = middle(power2)
    count = lax.axis_size(Z_AXIS)
    power3, rows = call(
        fourth_kernel,
        [field_shape, ((count, 128), f32)],
        [core, *got, planes, sent, volume, index, meta, maps, power0, power1, power2],
        scratch,
        scalars=1,
    )
    rows = sum_over(rows, Z_AXIS)
    (rows,) = call(repeat_sum_kernel, [((lax.axis_size(OTHERS), 128), f32)], [rows])
    rows = sum_over(rows, OTHERS)
    shape = (right_side.shape, f32)
    return tuple(
        call(last_kernel, [shape, shape], [rows, power0, power1, power2, power3])
    )


def solution(mesh):
    chips, cores = mesh.shape["sfc"], mesh.shape["grp"]
    sizes = (4, 4, chips // 16) if chips % 16 == 0 else (1, 1, chips)
    finer = Mesh(mesh.devices.reshape(*sizes, cores), SFC_GRP)
    split_cells = P(SFC_GRP)
    in_specs = (P(None, None, None, SFC_GRP),) + (split_cells,) * 7 + (P(),)
    out_specs = (P(None, None, None, SFC_GRP), P(None, None, None, SFC_GRP))
    return jax.shard_map(body, mesh=finer, in_specs=in_specs, out_specs=out_specs, check_vma=False)
```

```python
import functools

import jax
import jax.numpy as jnp
import numpy as np
from jax import lax
from jax.experimental import pallas as pl
from jax.experimental.pallas import tpu as pltpu
from jax.sharding import Mesh
from jax.sharding import PartitionSpec as P

NODES = 5
WIDTH = 25
CELLS = 128
GHOST = 96
ITERS = 3
SIGMA = 32.0
MASS_SHIFT = 1.0
Z_AXIS = ("sfc_2",)
OTHERS = ("sfc_0", "sfc_1", "grp")
SFC = ("sfc_0", "sfc_1", "sfc_2")
SFC_GRP = ("sfc_0", "sfc_1", "sfc_2", "grp")
VMEM_LIMIT = 24 * 1024 * 1024

f32 = jnp.float32
bf16 = jnp.bfloat16
highest = lax.Precision.HIGHEST


def node_tables():
    points = np.array([-1.0, -np.sqrt(3.0 / 7.0), 0.0, np.sqrt(3.0 / 7.0), 1.0])
    weights = np.array([0.1, 49.0 / 90.0, 32.0 / 45.0, 49.0 / 90.0, 0.1])
    identity = np.eye(5)
    spacing = points[:, None] - points[None, :] + identity
    barycentric = 1.0 / np.prod(spacing, axis=1)
    offdiag = barycentric[None, :] / barycentric[:, None] / spacing
    diagonal = np.sum(1.0 / spacing, axis=1) - 1.0
    derivs = np.where(identity > 0.5, diagonal[:, None], offdiag)
    stiffness = derivs.T @ (weights[:, None] * derivs)
    return stiffness, weights


STIFFNESS, WEIGHTS = node_tables()
FACE_MASS = [float(WEIGHTS[t // 5] * WEIGHTS[t % 5]) for t in range(WIDTH)]


def volume_tables():
    mass = np.diag(WEIGHTS)
    grads = (
        np.kron(np.kron(STIFFNESS, mass), mass)
        + np.kron(np.kron(mass, STIFFNESS), mass)
        + np.kron(np.kron(mass, mass), STIFFNESS)
    )
    full = np.zeros((128, 128), np.float32)
    full[:125, :125] = grads
    column = np.zeros((128, 128), np.float32)
    column[:125] = np.diag(np.kron(np.kron(mass, mass), mass))[:, None] * MASS_SHIFT
    return full, column


def face_node(face, t):
    high, low = t // 5, t % 5
    side = 4 * (face % 2)
    if face < 2:
        return 25 * side + t
    if face < 4:
        return 25 * high + 5 * side + low
    return 25 * high + 5 * low + side


def split(value):
    first = value.astype(bf16).astype(f32)
    rest = value - first
    second = rest.astype(bf16).astype(f32)
    third = (rest - second).astype(bf16).astype(f32)
    return first, second, third


def rev_first(planes, mask):
    return [jnp.where(mask, planes[5 * (4 - t // 5) + t % 5], planes[t]) for t in range(WIDTH)]


def rev_second(planes, mask):
    return [jnp.where(mask, planes[5 * (t // 5) + 4 - t % 5], planes[t]) for t in range(WIDTH)]


def swap(planes, mask):
    return [jnp.where(mask, planes[5 * (t % 5) + t // 5], planes[t]) for t in range(WIDTH)]


def orient_masks(codes):
    codes = codes.astype(jnp.int32)
    return (codes & 1) == 1, (codes & 2) == 2, (codes & 4) == 4


def orient_forward(planes, masks):
    return swap(rev_second(rev_first(planes, masks[0]), masks[1]), masks[2])


def orient_back(planes, masks):
    return rev_first(rev_second(swap(planes, masks[2]), masks[1]), masks[0])


def read_planes(ref, count=WIDTH):
    return [ref[8 * t : 8 * t + 8, :] for t in range(count)]


def gather_planes(field, face, cell):
    rows = {}

    def at(node):
        if node not in rows:
            row = jnp.broadcast_to(field[node : node + 1, :], (8, 128))
            rows[node] = jnp.take_along_axis(row, cell, axis=1, mode="promise_in_bounds")
        return rows[node]

    masks = [face == k for k in range(5)]
    planes = []
    for t in range(WIDTH):
        value = at(face_node(5, t))
        for k in range(5):
            value = jnp.where(masks[k], at(face_node(k, t)), value)
        planes.append(value)
    return planes


def write_messages(source, both_ref, up_ref, down_ref):
    def pair(ref, start, sent, own):
        ref[pl.ds(start, 28, stride=2), :] = source[pl.ds(4 + sent, 28, stride=8), :]
        ref[pl.ds(start + 1, 28, stride=2), :] = source[pl.ds(own, 28, stride=8), :]

    pair(both_ref, 0, 0, 1)
    pair(both_ref, 56, 1, 0)
    pair(up_ref, 0, 2, 3)
    pair(down_ref, 0, 3, 2)


def first_kernel(
    rhs_hbm,
    level_hbm,
    own_hbm,
    near_hbm,
    kind_hbm,
    orient_hbm,
    penalty_hbm,
    send_hbm,
    grads_hbm,
    mass_hbm,
    field_ref,
    planes_ref,
    index_ref,
    scale_ref,
    grads_ref,
    mass_ref,
    both_ref,
    up_ref,
    down_ref,
    rhs_ref,
    level_ref,
    own_ref,
    near_ref,
    kind_ref,
    orient_ref,
    penalty_ref,
    send_ref,
    sems,
):
    copies = [
        pltpu.make_async_copy(source, target, sems.at[k])
        for k, (source, target) in enumerate(
            (
                (own_hbm, own_ref.at[0]),
                (near_hbm, near_ref.at[0]),
                (kind_hbm, kind_ref.at[0]),
                (orient_hbm, orient_ref.at[0]),
                (penalty_hbm, penalty_ref.at[0]),
                (send_hbm, send_ref.at[0]),
                (level_hbm, level_ref.at[0]),
                (rhs_hbm, rhs_ref),
                (grads_hbm, grads_ref),
                (mass_hbm, mass_ref),
            )
        )
    ]
    for copy in copies:
        copy.start()
    for copy in copies:
        copy.wait()
    for a in range(5):
        for b in range(5):
            field_ref[25 * a + 5 * b : 25 * a + 5 * b + 5, :] = rhs_ref[a, b]
    field_ref[125:128, :] = jnp.zeros((3, 128), f32)
    own = own_ref[...]
    pieces = split(penalty_ref[...])
    rows = [
        (own >> 7).astype(f32),
        (own & 127).astype(f32),
        kind_ref[...].astype(f32),
        orient_ref[...].astype(f32),
        pieces[0],
        pieces[1],
        pieces[2],
        jnp.zeros((1, 384), f32),
    ]
    table = jnp.concatenate(rows, axis=0).astype(bf16)
    spot = lax.broadcasted_iota(jnp.int32, (512, 384), 0)
    lane = spot & 127
    wanted = jnp.where(lane < GHOST, 6 * CELLS + (spot >> 7) * GHOST + lane, -1)
    onehot = jnp.where(wanted == near_ref[...], 1.0, 0.0).astype(bf16)
    moved = lax.dot_general(
        table, onehot, (((1,), (1,)), ((), ())), preferred_element_type=f32
    )
    zeros = jnp.zeros((4, 128), f32)

    def upper(row):
        parts = [row[:, 128 * k : 128 * k + 128] for k in range(4)]
        return jnp.concatenate(parts + [zeros], axis=0)

    own_face, own_cell = upper(moved[0:1]), upper(moved[1:2])
    penalty = upper(moved[4:5] + moved[5:6] + moved[6:7])
    lanes = lax.broadcasted_iota(jnp.int32, (1, 128), 1)
    send = [
        jnp.where(lanes < GHOST, pltpu.roll(send_ref[...], (384 - GHOST * k) % 384, 1)[:, :128], 0)
        for k in range(4)
    ]
    send = jnp.concatenate([jnp.zeros((4, 128), jnp.int32)] + send, axis=0)
    sub = lax.broadcasted_iota(jnp.int32, (8, 128), 0)
    face = jnp.where(sub < 4, own_face.astype(jnp.int32), send >> 7)
    cell = jnp.where(sub < 4, own_cell.astype(jnp.int32), send & 127)
    index_ref[0:8, :] = face
    index_ref[8:16, :] = cell
    scale = jnp.exp2(-jnp.broadcast_to(level_ref[...], (8, 128)).astype(f32))
    scale_ref[...] = scale
    scaled = penalty * jnp.take_along_axis(scale, cell, axis=1, mode="promise_in_bounds")
    for t, plane in enumerate(gather_planes(field_ref, face, cell)):
        planes_ref[8 * t : 8 * t + 8, :] = plane
    planes_ref[200:208, :] = upper(moved[2:3])
    planes_ref[208:216, :] = upper(moved[3:4])
    planes_ref[216:224, :] = scaled
    write_messages(planes_ref, both_ref, up_ref, down_ref)


def local_volume(field, scale_ref, grads_ref, mass_ref):
    scale = scale_ref[0:1, :]
    grads = jnp.dot(grads_ref[...], field, precision=highest, preferred_element_type=f32)
    return scale * grads + (scale * scale * scale) * (mass_ref[...] * field)


def volume_kernel(
    field_ref,
    scale_ref,
    grads_ref,
    mass_ref,
    subface_hbm,
    volume_ref,
    plain_ref,
    turned_ref,
    subface_ref,
    sem,
):
    copy = pltpu.make_async_copy(subface_hbm, subface_ref, sem)
    copy.start()
    volume_ref[...] = local_volume(field_ref[...], scale_ref, grads_ref, mass_ref)
    plain_ref[...] = jnp.zeros((640, 128), f32)
    turned_ref[...] = jnp.zeros((640, 128), f32)
    copy.wait()
    lane = lax.broadcasted_iota(jnp.int32, (4, WIDTH), 1)
    sub = lax.broadcasted_iota(jnp.int32, (4, WIDTH), 0)
    for i in range(WIDTH):
        unit = jnp.where((lane == i) & (sub == 0), 1.0, 0.0)
        rows = jnp.concatenate([subface_ref[i], unit], axis=0)
        rows = jnp.concatenate(split(rows), axis=0)
        columns = jnp.transpose(rows)
        plain_ref[25 * i : 25 * i + 25, 0:24] = columns
        turned_ref[pl.ds(i, 25, stride=25), 0:24] = columns


def map_sent(maps_ref, planes_ref, meta_ref, masks):
    turned = orient_forward(read_planes(planes_ref), masks)
    result = []
    for i in range(WIDTH):
        total = None
        for j in range(WIDTH):
            at = 8 * (WIDTH * j + i)
            term = maps_ref[at : at + 8, :] * turned[j]
            total = term if total is None else total + term
        result.append(total)
    return result


def middle_kernel(
    field_ref, scale_ref, grads_ref, mass_ref, maps_ref, planes_ref, meta_ref, volume_ref, sent_ref
):
    volume_ref[...] = local_volume(field_ref[...], scale_ref, grads_ref, mass_ref)
    masks = orient_masks(meta_ref[8:16, :])
    for t, plane in enumerate(map_sent(maps_ref, planes_ref, meta_ref, masks)):
        sent_ref[8 * t : 8 * t + 8, :] = plane


def read_messages(core_ref, partner_ref, below_ref, above_ref, got_ref):
    low = core_ref[0] == 0

    def rows(ref, start):
        return ref[pl.ds(start, 28, stride=2), :]

    def put(row, value):
        got_ref[pl.ds(row, 28, stride=8), :] = value

    for j, (from_below, from_above) in enumerate(((0, 1), (5, 4))):
        put(from_below, jnp.where(low, rows(below_ref, 56 + j), rows(partner_ref, j)))
        put(from_above, jnp.where(low, rows(partner_ref, 56 + j), rows(above_ref, 56 + j)))
    put(2, rows(below_ref, 0))
    put(7, rows(below_ref, 1))
    put(3, rows(above_ref, 0))
    put(6, rows(above_ref, 1))


def build_maps(plain_ref, turned_ref, kind, maps_ref):
    code = lax.broadcasted_iota(jnp.int32, (8, 128), 0)
    code = jnp.where(code < 4, code + 2, jnp.where(code == 4, 1, -1)).astype(f32)
    for half, table_ref in enumerate((plain_ref, turned_ref)):
        table = table_ref[...].astype(bf16)
        chosen = []
        for row in range(4 * half, 4 * half + 4):
            chosen.append(jnp.where(code == kind[row : row + 1, :], 1.0, 0.0))
        chosen = jnp.concatenate(chosen, axis=1)
        unused = jnp.zeros((104, 512), f32)
        chosen = jnp.concatenate([chosen] * 3 + [unused], axis=0).astype(bf16)
        values = jnp.dot(table, chosen, preferred_element_type=f32)
        for k in range(4):
            maps_ref[pl.ds(4 * half + k, 640, stride=8), :] = values[:, 128 * k : 128 * k + 128]


def add_faces(volume_ref, planes, index_ref, pieces_ref, field_ref):
    for t, plane in enumerate(planes):
        pieces_ref[8 * t : 8 * t + 8, :] = plane
    pieces_ref[200:256, :] = jnp.zeros((56, 128), f32)
    face, cell = index_ref[0:8, :], index_ref[8:16, :]
    key = (face & 1) * 128 + cell
    axis = face >> 1
    slot = lax.broadcasted_iota(jnp.int32, (256, 128), 0)
    left, right = [], []
    for row in range(8):
        value = jnp.concatenate(split(pieces_ref[pl.ds(row, 32, stride=8), :]), axis=0)
        chosen = axis[row : row + 1, :]
        left.append(
            jnp.concatenate([jnp.where(chosen == k, value, 0.0) for k in range(3)], axis=0).astype(
                bf16
            )
        )
        right.append(jnp.where(slot == key[row : row + 1, :], 1.0, 0.0).astype(bf16))
    total = lax.dot_general(
        jnp.concatenate(left, axis=1),
        jnp.concatenate(right, axis=1),
        (((1,), (1,)), ((), ())),
        preferred_element_type=f32,
    )
    total = total * (1.0 / SIGMA)
    field_ref[...] = volume_ref[...] * (1.0 / SIGMA)
    for k in range(3):
        part = total[96 * k : 96 * k + 32] + total[96 * k + 32 : 96 * k + 64]
        part = part + total[96 * k + 64 : 96 * k + 96]
        for side in range(2):
            value = part[:WIDTH, 128 * side : 128 * side + 128]
            if k == 0:
                field_ref[100 * side : 100 * side + 25, :] += value
            elif k == 1:
                for a in range(5):
                    at = 25 * a + 20 * side
                    field_ref[at : at + 5, :] += value[5 * a : 5 * a + 5]
            else:
                field_ref[pl.ds(4 * side, 25, stride=5), :] += value


def combine(got_ref, planes_ref, sent, maps_ref, penalty, masks):
    sub = lax.broadcasted_iota(jnp.int32, (8, 128), 0)
    owned = sub < 4
    got = read_planes(got_ref)
    turned = orient_forward(got, masks)
    mixed = [
        jnp.where(owned, turned[t], (penalty * FACE_MASS[t]) * (got[t] - sent[t]))
        for t in range(WIDTH)
    ]
    mapped = []
    for i in range(WIDTH):
        total = None
        for j in range(WIDTH):
            at = 8 * (WIDTH * i + j)
            term = maps_ref[at : at + 8, :] * mixed[j]
            total = term if total is None else total + term
        mapped.append(total)
    back = orient_back(mapped, masks)
    return [
        jnp.where(
            owned,
            (penalty * FACE_MASS[t]) * (planes_ref[8 * t : 8 * t + 8, :] - mapped[t]),
            -back[t],
        )
        for t in range(WIDTH)
    ]


def next_messages(field_ref, index_ref, planes_ref, both_ref, up_ref, down_ref):
    face, cell = index_ref[0:8, :], index_ref[8:16, :]
    for t, plane in enumerate(gather_planes(field_ref, face, cell)):
        planes_ref[8 * t : 8 * t + 8, :] = plane
    planes_ref[200:224, :] = jnp.zeros((24, 128), f32)
    write_messages(planes_ref, both_ref, up_ref, down_ref)


def second_kernel(
    core_ref,
    partner_ref,
    below_ref,
    above_ref,
    old_ref,
    volume_ref,
    index_ref,
    plain_ref,
    turned_ref,
    field_ref,
    planes_ref,
    meta_ref,
    maps_ref,
    both_ref,
    up_ref,
    down_ref,
    got_ref,
    pieces_ref,
):
    read_messages(core_ref, partner_ref, below_ref, above_ref, got_ref)
    sub = lax.broadcasted_iota(jnp.int32, (8, 128), 0)
    for k in range(3):
        at = 200 + 8 * k
        meta_ref[8 * k : 8 * k + 8, :] = jnp.where(
            sub < 4, old_ref[at : at + 8, :], got_ref[at : at + 8, :]
        )
    masks = orient_masks(meta_ref[8:16, :])
    build_maps(plain_ref, turned_ref, meta_ref[0:8, :], maps_ref)
    sent = map_sent(maps_ref, old_ref, meta_ref, masks)
    planes = combine(got_ref, old_ref, sent, maps_ref, meta_ref[16:24, :], masks)
    add_faces(volume_ref, planes, index_ref, pieces_ref, field_ref)
    next_messages(field_ref, index_ref, planes_ref, both_ref, up_ref, down_ref)


def third_kernel(
    core_ref,
    partner_ref,
    below_ref,
    above_ref,
    old_ref,
    sent_ref,
    volume_ref,
    index_ref,
    meta_ref,
    maps_ref,
    field_ref,
    planes_ref,
    both_ref,
    up_ref,
    down_ref,
    got_ref,
    pieces_ref,
):
    read_messages(core_ref, partner_ref, below_ref, above_ref, got_ref)
    masks = orient_masks(meta_ref[8:16, :])
    sent = read_planes(sent_ref)
    planes = combine(got_ref, old_ref, sent, maps_ref, meta_ref[16:24, :], masks)
    add_faces(volume_ref, planes, index_ref, pieces_ref, field_ref)
    next_messages(field_ref, index_ref, planes_ref, both_ref, up_ref, down_ref)


def fourth_kernel(
    core_ref,
    partner_ref,
    below_ref,
    above_ref,
    old_ref,
    sent_ref,
    volume_ref,
    index_ref,
    meta_ref,
    maps_ref,
    power0_ref,
    power1_ref,
    power2_ref,
    field_ref,
    moments_ref,
    got_ref,
    pieces_ref,
):
    read_messages(core_ref, partner_ref, below_ref, above_ref, got_ref)
    masks = orient_masks(meta_ref[8:16, :])
    sent = read_planes(sent_ref)
    planes = combine(got_ref, old_ref, sent, maps_ref, meta_ref[16:24, :], masks)
    add_faces(volume_ref, planes, index_ref, pieces_ref, field_ref)
    powers = [power0_ref[...], power1_ref[...], power2_ref[...], field_ref[...]]
    lane = lax.broadcasted_iota(jnp.int32, (1, 128), 1)
    result = jnp.zeros((1, 128), f32)
    for k in range(2 * ITERS):
        row = jnp.sum(powers[k // 2] * powers[(k + 1) // 2], axis=0, keepdims=True)
        result = jnp.where(lane == k, jnp.sum(row, axis=1, keepdims=True), result)
    moments_ref[...] = jnp.broadcast_to(result, moments_ref.shape)


def repeat_sum_kernel(rows_ref, out_ref):
    total = jnp.sum(rows_ref[...], axis=0, keepdims=True)
    out_ref[...] = jnp.broadcast_to(total, out_ref.shape)


def coefficients(moments):
    def inner(one, two, shift):
        total = None
        for i in range(len(one)):
            for j in range(len(two)):
                term = one[i] * two[j] * moments[i + j + shift]
                total = term if total is None else total + term
        return total

    unit = jnp.ones_like(moments[0])
    none = jnp.zeros_like(moments[0])
    iterate, remains, search = [], [unit], [unit]
    norm_now = moments[0]
    for iteration in range(ITERS):
        step = norm_now / inner(search, search, 1)
        iterate = [
            (iterate[i] if i < len(iterate) else none) + step * search[i]
            for i in range(len(search))
        ]
        image = [none] + search
        remains = [
            (remains[i] if i < len(remains) else none) - step * image[i]
            for i in range(len(image))
        ]
        if iteration + 1 < ITERS:
            norm_next = inner(remains, remains, 0)
            blend = norm_next / norm_now
            search = [
                remains[i] + (blend * search[i] if i < len(search) else none)
                for i in range(len(remains))
            ]
            norm_now = norm_next
    return iterate, remains


def last_kernel(
    rows_ref, power0_ref, power1_ref, power2_ref, power3_ref, solution_ref, residual_ref
):
    total = jnp.sum(rows_ref[...], axis=0, keepdims=True)
    lane = lax.broadcasted_iota(jnp.int32, (1, 128), 1)
    moments = [
        jnp.broadcast_to(
            jnp.sum(jnp.where(lane == k, total, 0.0), axis=1, keepdims=True), (1, 128)
        )
        for k in range(2 * ITERS)
    ]
    iterate, remains = coefficients(moments)
    powers = (power0_ref, power1_ref, power2_ref, power3_ref)
    for a in range(5):
        for b in range(5):
            at = 25 * a + 5 * b
            values = [ref[at : at + 5, :] for ref in powers]
            answer = sum((c * (1.0 / SIGMA)) * v for c, v in zip(iterate, values))
            solution_ref[a, b] = answer
            residual_ref[a, b] = sum(c * v for c, v in zip(remains, values))


def call(kernel, outs, ins, scratch=(), places=None, flops=0):
    places = places or {}
    ins = [
        pltpu.with_memory_space_constraint(x, pltpu.HBM) if places.get(k) is pltpu.HBM else x
        for k, x in enumerate(ins)
    ]
    in_specs = [pl.BlockSpec(memory_space=places.get(k, pltpu.VMEM)) for k in range(len(ins))]
    return pl.pallas_call(
        kernel,
        out_shape=[jax.ShapeDtypeStruct(shape, kind) for shape, kind in outs],
        in_specs=in_specs,
        out_specs=[pl.BlockSpec(memory_space=pltpu.VMEM)] * len(outs),
        scratch_shapes=list(scratch),
        compiler_params=pltpu.CompilerParams(vmem_limit_bytes=VMEM_LIMIT),
        cost_estimate=pl.CostEstimate(flops=flops, bytes_accessed=0, transcendentals=0),
    )(*ins)


def shifted(block, axis, distance):
    devices = range(lax.axis_size(axis))
    route = [(i - distance, i) for i in devices if i - distance in devices]
    return lax.ppermute(block, axis, route)


def exchange(both, up, down):
    partner = lax.ppermute(both, "grp", [(0, 1), (1, 0)])
    below = shifted(jnp.concatenate([up, partner[:56]], axis=0), SFC, 1)
    above = shifted(jnp.concatenate([down, partner[56:]], axis=0), SFC, -1)
    return partner, below, above


def sum_over(rows, axes):
    return lax.all_to_all(rows, axes, 0, 0, tiled=True)


def body(
    right_side,
    cell_level,
    own_slot,
    near_slot,
    face_kind,
    orientation,
    penalty,
    send_slots,
    subface_maps,
):
    field_shape, planes_shape = ((128, 128), f32), ((256, 128), f32)
    messages = [((112, 128), f32), ((56, 128), f32), ((56, 128), f32)]
    core = lax.axis_index("grp").astype(jnp.int32).reshape(1)
    tables = [jnp.asarray(table) for table in volume_tables()]
    row, whole = ((1, 384), jnp.int32), ((128, 128), f32)
    power0, planes, index, scale, grads, mass, *sends = call(
        first_kernel,
        [field_shape, planes_shape, ((16, 128), jnp.int32), ((8, 128), f32), whole, whole] + messages,
        [right_side, cell_level, own_slot, near_slot, face_kind, orientation, penalty, send_slots]
        + tables,
        [pltpu.VMEM(right_side.shape, f32), pltpu.VMEM((1, 128), jnp.int32)]
        + [pltpu.VMEM(*row)] * 4
        + [pltpu.VMEM((1, 384), f32), pltpu.VMEM(*row), pltpu.SemaphoreType.DMA((10,))],
        {k: pltpu.HBM for k in range(10)},
    )
    scratch = [pltpu.VMEM((224, 128), f32), pltpu.VMEM((256, 128), f32)]
    got = exchange(*sends)
    volume, plain, turned = call(
        volume_kernel,
        [field_shape, ((640, 128), f32), ((640, 128), f32)],
        [power0, scale, grads, mass, jnp.transpose(subface_maps, (1, 0, 2))],
        [pltpu.VMEM((WIDTH, 4, WIDTH), f32), pltpu.SemaphoreType.DMA],
        {4: pltpu.HBM},
        flops=10**7,
    )
    power1, new_planes, meta, maps, *sends = call(
        second_kernel,
        [field_shape, planes_shape, ((24, 128), f32), ((5120, 128), f32)] + messages,
        [core, *got, planes, volume, index, plain, turned],
        scratch,
        {0: pltpu.SMEM},
    )
    planes = new_planes

    def middle(field):
        return call(
            middle_kernel,
            [field_shape, planes_shape],
            [field, scale, grads, mass, maps, planes, meta],
            flops=10**7,
        )

    got = exchange(*sends)
    volume, sent = middle(power1)
    power2, new_planes, *sends = call(
        third_kernel,
        [field_shape, planes_shape] + messages,
        [core, *got, planes, sent, volume, index, meta, maps],
        scratch,
        {0: pltpu.SMEM},
    )
    planes = new_planes
    got = exchange(*sends)
    volume, sent = middle(power2)
    count = lax.axis_size(Z_AXIS)
    power3, rows = call(
        fourth_kernel,
        [field_shape, ((count, 128), f32)],
        [core, *got, planes, sent, volume, index, meta, maps, power0, power1, power2],
        scratch,
        {0: pltpu.SMEM},
    )
    rows = sum_over(rows, Z_AXIS)
    (rows,) = call(repeat_sum_kernel, [((lax.axis_size(OTHERS), 128), f32)], [rows])
    rows = sum_over(rows, OTHERS)
    shape = (right_side.shape, f32)
    return tuple(
        call(last_kernel, [shape, shape], [rows, power0, power1, power2, power3])
    )


def solution(mesh):
    chips, cores = mesh.shape["sfc"], mesh.shape["grp"]
    sizes = (4, 4, chips // 16) if chips % 16 == 0 else (1, 1, chips)
    finer = Mesh(mesh.devices.reshape(*sizes, cores), SFC_GRP)
    split_cells = P(SFC_GRP)
    in_specs = (P(None, None, None, SFC_GRP),) + (split_cells,) * 7 + (P(),)
    out_specs = (P(None, None, None, SFC_GRP), P(None, None, None, SFC_GRP))
    return jax.shard_map(body, mesh=finer, in_specs=in_specs, out_specs=out_specs, check_vma=False)
```

```python
import functools

import jax
import jax.numpy as jnp
import numpy as np
from jax import lax
from jax.experimental import pallas as pl
from jax.experimental.pallas import tpu as pltpu
from jax.sharding import Mesh
from jax.sharding import PartitionSpec as P

NODES = 5
WIDTH = 25
CELLS = 128
GHOST = 96
ITERS = 3
SIGMA = 32.0
MASS_SHIFT = 1.0
Z_AXIS = ("sfc_2",)
OTHERS = ("sfc_0", "sfc_1")
SFC = ("sfc_0", "sfc_1", "sfc_2")
SFC_GRP = ("sfc_0", "sfc_1", "sfc_2", "grp")
VMEM_LIMIT = 24 * 1024 * 1024

f32 = jnp.float32
bf16 = jnp.bfloat16
highest = lax.Precision.HIGHEST


def node_tables():
    points = np.array([-1.0, -np.sqrt(3.0 / 7.0), 0.0, np.sqrt(3.0 / 7.0), 1.0])
    weights = np.array([0.1, 49.0 / 90.0, 32.0 / 45.0, 49.0 / 90.0, 0.1])
    identity = np.eye(5)
    spacing = points[:, None] - points[None, :] + identity
    barycentric = 1.0 / np.prod(spacing, axis=1)
    offdiag = barycentric[None, :] / barycentric[:, None] / spacing
    diagonal = np.sum(1.0 / spacing, axis=1) - 1.0
    derivs = np.where(identity > 0.5, diagonal[:, None], offdiag)
    stiffness = derivs.T @ (weights[:, None] * derivs)
    return stiffness, weights


STIFFNESS, WEIGHTS = node_tables()
FACE_MASS = [float(WEIGHTS[t // 5] * WEIGHTS[t % 5]) for t in range(WIDTH)]


def volume_tables():
    mass = np.diag(WEIGHTS)
    grads = (
        np.kron(np.kron(STIFFNESS, mass), mass)
        + np.kron(np.kron(mass, STIFFNESS), mass)
        + np.kron(np.kron(mass, mass), STIFFNESS)
    )
    full = np.zeros((128, 128), np.float32)
    full[:125, :125] = grads
    column = np.zeros((128, 128), np.float32)
    column[:125] = np.diag(np.kron(np.kron(mass, mass), mass))[:, None] * MASS_SHIFT
    return full, column


def face_node(face, t):
    high, low = t // 5, t % 5
    side = 4 * (face % 2)
    if face < 2:
        return 25 * side + t
    if face < 4:
        return 25 * high + 5 * side + low
    return 25 * high + 5 * low + side


def split(value):
    first = value.astype(bf16).astype(f32)
    rest = value - first
    second = rest.astype(bf16).astype(f32)
    third = (rest - second).astype(bf16).astype(f32)
    return first, second, third


def rev_first(planes, mask):
    return [jnp.where(mask, planes[5 * (4 - t // 5) + t % 5], planes[t]) for t in range(WIDTH)]


def rev_second(planes, mask):
    return [jnp.where(mask, planes[5 * (t // 5) + 4 - t % 5], planes[t]) for t in range(WIDTH)]


def swap(planes, mask):
    return [jnp.where(mask, planes[5 * (t % 5) + t // 5], planes[t]) for t in range(WIDTH)]


def orient_masks(codes):
    codes = codes.astype(jnp.int32)
    return (codes & 1) == 1, (codes & 2) == 2, (codes & 4) == 4


def orient_forward(planes, masks):
    return swap(rev_second(rev_first(planes, masks[0]), masks[1]), masks[2])


def orient_back(planes, masks):
    return rev_first(rev_second(swap(planes, masks[2]), masks[1]), masks[0])


def read_planes(ref, count=WIDTH):
    return [ref[8 * t : 8 * t + 8, :] for t in range(count)]


def gather_planes(field, face, cell):
    rows = {}

    def at(node):
        if node not in rows:
            row = jnp.broadcast_to(field[node : node + 1, :], (8, 128))
            rows[node] = jnp.take_along_axis(row, cell, axis=1, mode="promise_in_bounds")
        return rows[node]

    masks = [face == k for k in range(5)]
    planes = []
    for t in range(WIDTH):
        value = at(face_node(5, t))
        for k in range(5):
            value = jnp.where(masks[k], at(face_node(k, t)), value)
        planes.append(value)
    return planes


def write_messages(sources, up_ref, down_ref):
    def pair(ref, start, source, sent, own):
        ref[pl.ds(start, 28, stride=2), :] = source[pl.ds(4 + sent, 28, stride=8), :]
        ref[pl.ds(start + 1, 28, stride=2), :] = source[pl.ds(own, 28, stride=8), :]

    for half in range(2):
        pair(up_ref, 56 * half, sources[half], 2, 3)
        pair(down_ref, 56 * half, sources[half], 3, 2)
    pair(up_ref, 112, sources[1], 0, 1)
    pair(down_ref, 112, sources[0], 1, 0)


def pack_kernel(
    rhs_hbm,
    level_hbm,
    own_hbm,
    near_hbm,
    kind_hbm,
    orient_hbm,
    penalty_hbm,
    send_hbm,
    raw_ref,
    rhs_ref,
    level_ref,
    own_ref,
    near_ref,
    kind_ref,
    orient_ref,
    penalty_ref,
    send_ref,
    sems,
):
    copies = [
        pltpu.make_async_copy(source, target, sems.at[k])
        for k, (source, target) in enumerate(
            (
                (own_hbm, own_ref.at[0]),
                (near_hbm, near_ref.at[0]),
                (kind_hbm, kind_ref.at[0]),
                (orient_hbm, orient_ref.at[0]),
                (penalty_hbm, penalty_ref.at[0]),
                (send_hbm, send_ref.at[0]),
                (level_hbm, level_ref.at[0]),
                (rhs_hbm, rhs_ref),
            )
        )
    ]
    for copy in copies:
        copy.start()
    for copy in copies:
        copy.wait()
    for a in range(5):
        for b in range(5):
            raw_ref[25 * a + 5 * b : 25 * a + 5 * b + 5, :] = rhs_ref[a, b]
    raw_ref[125:128, :] = jnp.zeros((3, 128), f32)
    for k, ref in enumerate((own_ref, near_ref, kind_ref, orient_ref, penalty_ref, send_ref)):
        for third in range(3):
            at = 128 + 3 * k + third
            raw_ref[at : at + 1, :] = ref[:, 128 * third : 128 * third + 128].astype(f32)
    raw_ref[146:147, :] = level_ref[...].astype(f32)
    raw_ref[147:152, :] = jnp.zeros((5, 128), f32)


def first_kernel(core_ref, mine_ref, other_ref, grads_hbm, mass_hbm, *refs):
    outs, (grads_ref, mass_ref, up_ref, down_ref, sems) = refs[:8], refs[8:]
    copies = [
        pltpu.make_async_copy(grads_hbm, grads_ref, sems.at[0]),
        pltpu.make_async_copy(mass_hbm, mass_ref, sems.at[1]),
    ]
    for copy in copies:
        copy.start()
    low = core_ref[0] == 0
    for half in range(2):
        first, second = (mine_ref, other_ref) if half == 0 else (other_ref, mine_ref)
        outs[4 * half][...] = jnp.where(low, first[0:128, :], second[0:128, :])
        raw = jnp.where(low, first[128:152, :], second[128:152, :])
        prepare_half(raw, *outs[4 * half : 4 * half + 4])
    write_messages((outs[1], outs[5]), up_ref, down_ref)
    for copy in copies:
        copy.wait()


def prepare_half(raw, field_ref, planes_ref, index_ref, scale_ref):
    def entries(k):
        return jnp.concatenate([raw[3 * k + third : 3 * k + third + 1] for third in range(3)], axis=1)

    own = entries(0).astype(jnp.int32)
    near = entries(1).astype(jnp.int32)
    pieces = split(entries(4))
    rows = [
        (own >> 7).astype(f32),
        (own & 127).astype(f32),
        entries(2),
        entries(3),
        pieces[0],
        pieces[1],
        pieces[2],
        jnp.zeros((1, 384), f32),
    ]
    table = jnp.concatenate(rows, axis=0).astype(bf16)
    spot = lax.broadcasted_iota(jnp.int32, (512, 384), 0)
    lane = spot & 127
    wanted = jnp.where(lane < GHOST, 6 * CELLS + (spot >> 7) * GHOST + lane, -1)
    onehot = jnp.where(wanted == near, 1.0, 0.0).astype(bf16)
    moved = lax.dot_general(
        table, onehot, (((1,), (1,)), ((), ())), preferred_element_type=f32
    )
    zeros = jnp.zeros((4, 128), f32)

    def upper(row):
        parts = [row[:, 128 * k : 128 * k + 128] for k in range(4)]
        return jnp.concatenate(parts + [zeros], axis=0)

    own_face, own_cell = upper(moved[0:1]), upper(moved[1:2])
    penalty = upper(moved[4:5] + moved[5:6] + moved[6:7])
    lanes = lax.broadcasted_iota(jnp.int32, (1, 128), 1)
    sends = entries(5).astype(jnp.int32)
    send = [
        jnp.where(lanes < GHOST, pltpu.roll(sends, (384 - GHOST * k) % 384, 1)[:, :128], 0)
        for k in range(4)
    ]
    send = jnp.concatenate([jnp.zeros((4, 128), jnp.int32)] + send, axis=0)
    sub = lax.broadcasted_iota(jnp.int32, (8, 128), 0)
    face = jnp.where(sub < 4, own_face.astype(jnp.int32), send >> 7)
    cell = jnp.where(sub < 4, own_cell.astype(jnp.int32), send & 127)
    index_ref[0:8, :] = face
    index_ref[8:16, :] = cell
    scale = jnp.exp2(-jnp.broadcast_to(raw[18:19], (8, 128)))
    scale_ref[...] = scale
    scaled = penalty * jnp.take_along_axis(scale, cell, axis=1, mode="promise_in_bounds")
    for t, plane in enumerate(gather_planes(field_ref, face, cell)):
        planes_ref[8 * t : 8 * t + 8, :] = plane
    planes_ref[200:208, :] = upper(moved[2:3])
    planes_ref[208:216, :] = upper(moved[3:4])
    planes_ref[216:224, :] = scaled


def local_volume(field, scale_ref, grads_ref, mass_ref):
    scale = scale_ref[0:1, :]
    grads = jnp.dot(grads_ref[...], field, precision=highest, preferred_element_type=f32)
    return scale * grads + (scale * scale * scale) * (mass_ref[...] * field)


def volume_kernel(
    field0_ref,
    field1_ref,
    scale0_ref,
    scale1_ref,
    grads_ref,
    mass_ref,
    subface_hbm,
    volume0_ref,
    volume1_ref,
    plain_ref,
    turned_ref,
    subface_ref,
    sem,
):
    copy = pltpu.make_async_copy(subface_hbm, subface_ref, sem)
    copy.start()
    volume0_ref[...] = local_volume(field0_ref[...], scale0_ref, grads_ref, mass_ref)
    volume1_ref[...] = local_volume(field1_ref[...], scale1_ref, grads_ref, mass_ref)
    plain_ref[...] = jnp.zeros((640, 128), f32)
    turned_ref[...] = jnp.zeros((640, 128), f32)
    copy.wait()
    lane = lax.broadcasted_iota(jnp.int32, (4, WIDTH), 1)
    sub = lax.broadcasted_iota(jnp.int32, (4, WIDTH), 0)
    for i in range(WIDTH):
        unit = jnp.where((lane == i) & (sub == 0), 1.0, 0.0)
        rows = jnp.concatenate([subface_ref[i], unit], axis=0)
        rows = jnp.concatenate(split(rows), axis=0)
        columns = jnp.transpose(rows)
        plain_ref[25 * i : 25 * i + 25, 0:24] = columns
        turned_ref[pl.ds(i, 25, stride=25), 0:24] = columns


def map_sent(maps_ref, planes_ref, meta_ref, masks):
    turned = orient_forward(read_planes(planes_ref), masks)
    result = []
    for i in range(WIDTH):
        total = None
        for j in range(WIDTH):
            at = 8 * (WIDTH * j + i)
            term = maps_ref[at : at + 8, :] * turned[j]
            total = term if total is None else total + term
        result.append(total)
    return result


def middle_kernel(grads_ref, mass_ref, *refs):
    for half in range(2):
        field_ref, scale_ref, maps_ref, planes_ref, meta_ref = refs[5 * half : 5 * half + 5]
        volume_ref, sent_ref = refs[10 + 2 * half : 12 + 2 * half]
        volume_ref[...] = local_volume(field_ref[...], scale_ref, grads_ref, mass_ref)
        masks = orient_masks(meta_ref[8:16, :])
        for t, plane in enumerate(map_sent(maps_ref, planes_ref, meta_ref, masks)):
            sent_ref[8 * t : 8 * t + 8, :] = plane


def read_messages(below_ref, above_ref, sources, gots):
    def put(half, row, value):
        gots[half][pl.ds(row, 28, stride=8), :] = value

    def rows(ref, start):
        return ref[pl.ds(start, 28, stride=2), :]

    def local(half, row):
        return sources[half][pl.ds(row, 28, stride=8), :]

    for half in range(2):
        put(half, 2, rows(below_ref, 56 * half))
        put(half, 7, rows(below_ref, 56 * half + 1))
        put(half, 3, rows(above_ref, 56 * half))
        put(half, 6, rows(above_ref, 56 * half + 1))
    put(0, 0, rows(below_ref, 112))
    put(0, 5, rows(below_ref, 113))
    put(1, 1, rows(above_ref, 112))
    put(1, 4, rows(above_ref, 113))
    put(0, 1, local(1, 5))
    put(0, 4, local(1, 0))
    put(1, 0, local(0, 4))
    put(1, 5, local(0, 1))


def build_maps(plain_ref, turned_ref, kind, maps_ref):
    code = lax.broadcasted_iota(jnp.int32, (8, 128), 0)
    code = jnp.where(code < 4, code + 2, jnp.where(code == 4, 1, -1)).astype(f32)
    for half, table_ref in enumerate((plain_ref, turned_ref)):
        table = table_ref[...].astype(bf16)
        chosen = []
        for row in range(4 * half, 4 * half + 4):
            chosen.append(jnp.where(code == kind[row : row + 1, :], 1.0, 0.0))
        chosen = jnp.concatenate(chosen, axis=1)
        unused = jnp.zeros((104, 512), f32)
        chosen = jnp.concatenate([chosen] * 3 + [unused], axis=0).astype(bf16)
        values = jnp.dot(table, chosen, preferred_element_type=f32)
        for k in range(4):
            maps_ref[pl.ds(4 * half + k, 640, stride=8), :] = values[:, 128 * k : 128 * k + 128]


def add_faces(volume_ref, planes, index_ref, pieces_ref, field_ref):
    for t, plane in enumerate(planes):
        pieces_ref[8 * t : 8 * t + 8, :] = plane
    pieces_ref[200:256, :] = jnp.zeros((56, 128), f32)
    face, cell = index_ref[0:8, :], index_ref[8:16, :]
    key = (face & 1) * 128 + cell
    axis = face >> 1
    slot = lax.broadcasted_iota(jnp.int32, (256, 128), 0)
    left, right = [], []
    for row in range(8):
        value = jnp.concatenate(split(pieces_ref[pl.ds(row, 32, stride=8), :]), axis=0)
        chosen = axis[row : row + 1, :]
        left.append(
            jnp.concatenate([jnp.where(chosen == k, value, 0.0) for k in range(3)], axis=0).astype(
                bf16
            )
        )
        right.append(jnp.where(slot == key[row : row + 1, :], 1.0, 0.0).astype(bf16))
    total = lax.dot_general(
        jnp.concatenate(left, axis=1),
        jnp.concatenate(right, axis=1),
        (((1,), (1,)), ((), ())),
        preferred_element_type=f32,
    )
    total = total * (1.0 / SIGMA)
    field_ref[...] = volume_ref[...] * (1.0 / SIGMA)
    for k in range(3):
        part = total[96 * k : 96 * k + 32] + total[96 * k + 32 : 96 * k + 64]
        part = part + total[96 * k + 64 : 96 * k + 96]
        for side in range(2):
            value = part[:WIDTH, 128 * side : 128 * side + 128]
            if k == 0:
                field_ref[100 * side : 100 * side + 25, :] += value
            elif k == 1:
                for a in range(5):
                    at = 25 * a + 20 * side
                    field_ref[at : at + 5, :] += value[5 * a : 5 * a + 5]
            else:
                field_ref[pl.ds(4 * side, 25, stride=5), :] += value


def combine(got_ref, planes_ref, sent, maps_ref, penalty, masks):
    sub = lax.broadcasted_iota(jnp.int32, (8, 128), 0)
    owned = sub < 4
    got = read_planes(got_ref)
    turned = orient_forward(got, masks)
    mixed = [
        jnp.where(owned, turned[t], (penalty * FACE_MASS[t]) * (got[t] - sent[t]))
        for t in range(WIDTH)
    ]
    mapped = []
    for i in range(WIDTH):
        total = None
        for j in range(WIDTH):
            at = 8 * (WIDTH * i + j)
            term = maps_ref[at : at + 8, :] * mixed[j]
            total = term if total is None else total + term
        mapped.append(total)
    back = orient_back(mapped, masks)
    return [
        jnp.where(
            owned,
            (penalty * FACE_MASS[t]) * (planes_ref[8 * t : 8 * t + 8, :] - mapped[t]),
            -back[t],
        )
        for t in range(WIDTH)
    ]


def next_planes(field_ref, index_ref, planes_ref):
    face, cell = index_ref[0:8, :], index_ref[8:16, :]
    for t, plane in enumerate(gather_planes(field_ref, face, cell)):
        planes_ref[8 * t : 8 * t + 8, :] = plane
    planes_ref[200:224, :] = jnp.zeros((24, 128), f32)


def second_kernel(below_ref, above_ref, plain_ref, turned_ref, *refs):
    ins, outs = (refs[0:3], refs[3:6]), (refs[6:10], refs[10:14])
    up_ref, down_ref, got0_ref, got1_ref, pieces_ref = refs[14:]
    gots = (got0_ref, got1_ref)
    read_messages(below_ref, above_ref, (ins[0][0], ins[1][0]), gots)
    sub = lax.broadcasted_iota(jnp.int32, (8, 128), 0)
    for half in range(2):
        old_ref, volume_ref, index_ref = ins[half]
        field_ref, planes_ref, meta_ref, maps_ref = outs[half]
        got_ref = gots[half]
        for k in range(3):
            at = 200 + 8 * k
            meta_ref[8 * k : 8 * k + 8, :] = jnp.where(
                sub < 4, old_ref[at : at + 8, :], got_ref[at : at + 8, :]
            )
        masks = orient_masks(meta_ref[8:16, :])
        build_maps(plain_ref, turned_ref, meta_ref[0:8, :], maps_ref)
        sent = map_sent(maps_ref, old_ref, meta_ref, masks)
        planes = combine(got_ref, old_ref, sent, maps_ref, meta_ref[16:24, :], masks)
        add_faces(volume_ref, planes, index_ref, pieces_ref, field_ref)
        next_planes(field_ref, index_ref, planes_ref)
    write_messages((outs[0][1], outs[1][1]), up_ref, down_ref)


def apply_half(got_ref, ins, pieces_ref, field_ref):
    old_ref, sent_ref, volume_ref, index_ref, meta_ref, maps_ref = ins
    masks = orient_masks(meta_ref[8:16, :])
    sent = read_planes(sent_ref)
    planes = combine(got_ref, old_ref, sent, maps_ref, meta_ref[16:24, :], masks)
    add_faces(volume_ref, planes, index_ref, pieces_ref, field_ref)


def third_kernel(below_ref, above_ref, *refs):
    ins, outs = (refs[0:6], refs[6:12]), (refs[12:14], refs[14:16])
    up_ref, down_ref, got0_ref, got1_ref, pieces_ref = refs[16:]
    gots = (got0_ref, got1_ref)
    read_messages(below_ref, above_ref, (ins[0][0], ins[1][0]), gots)
    for half in range(2):
        field_ref, planes_ref = outs[half]
        apply_half(gots[half], ins[half], pieces_ref, field_ref)
        next_planes(field_ref, ins[half][3], planes_ref)
    write_messages((outs[0][1], outs[1][1]), up_ref, down_ref)


def fourth_kernel(below_ref, above_ref, *refs):
    ins, old_powers = (refs[0:6], refs[6:12]), (refs[12:15], refs[15:18])
    fields, (moments_ref, got0_ref, got1_ref, pieces_ref) = refs[18:20], refs[20:]
    gots = (got0_ref, got1_ref)
    read_messages(below_ref, above_ref, (ins[0][0], ins[1][0]), gots)
    for half in range(2):
        apply_half(gots[half], ins[half], pieces_ref, fields[half])
    powers = [
        [ref[...] for ref in old_powers[half]] + [fields[half][...]] for half in range(2)
    ]
    lane = lax.broadcasted_iota(jnp.int32, (1, 128), 1)
    result = jnp.zeros((1, 128), f32)
    for k in range(2 * ITERS):
        both = sum(powers[half][k // 2] * powers[half][(k + 1) // 2] for half in range(2))
        row = jnp.sum(both, axis=0, keepdims=True)
        result = jnp.where(lane == k, jnp.sum(row, axis=1, keepdims=True), result)
    moments_ref[...] = jnp.broadcast_to(result, moments_ref.shape)


def repeat_sum_kernel(rows_ref, out_ref):
    total = jnp.sum(rows_ref[...], axis=0, keepdims=True)
    out_ref[...] = jnp.broadcast_to(total, out_ref.shape)


def coefficients(moments):
    def inner(one, two, shift):
        total = None
        for i in range(len(one)):
            for j in range(len(two)):
                term = one[i] * two[j] * moments[i + j + shift]
                total = term if total is None else total + term
        return total

    unit = jnp.ones_like(moments[0])
    none = jnp.zeros_like(moments[0])
    iterate, remains, search = [], [unit], [unit]
    norm_now = moments[0]
    for iteration in range(ITERS):
        step = norm_now / inner(search, search, 1)
        iterate = [
            (iterate[i] if i < len(iterate) else none) + step * search[i]
            for i in range(len(search))
        ]
        image = [none] + search
        remains = [
            (remains[i] if i < len(remains) else none) - step * image[i]
            for i in range(len(image))
        ]
        if iteration + 1 < ITERS:
            norm_next = inner(remains, remains, 0)
            blend = norm_next / norm_now
            search = [
                remains[i] + (blend * search[i] if i < len(search) else none)
                for i in range(len(remains))
            ]
            norm_now = norm_next
    return iterate, remains


def last_kernel(core_ref, rows_ref, *refs):
    halves, (solution_ref, residual_ref) = (refs[0:4], refs[4:8]), refs[8:]
    low = core_ref[0] == 0
    total = jnp.sum(rows_ref[...], axis=0, keepdims=True)
    lane = lax.broadcasted_iota(jnp.int32, (1, 128), 1)
    moments = [
        jnp.broadcast_to(
            jnp.sum(jnp.where(lane == k, total, 0.0), axis=1, keepdims=True), (1, 128)
        )
        for k in range(2 * ITERS)
    ]
    iterate, remains = coefficients(moments)
    for a in range(5):
        for b in range(5):
            at = 25 * a + 5 * b
            values = [
                jnp.where(low, one[at : at + 5, :], two[at : at + 5, :]) for one, two in zip(*halves)
            ]
            answer = sum((c * (1.0 / SIGMA)) * v for c, v in zip(iterate, values))
            solution_ref[a, b] = answer
            residual_ref[a, b] = sum(c * v for c, v in zip(remains, values))


def call(kernel, outs, ins, scratch=(), places=None, flops=0):
    places = places or {}
    ins = [
        pltpu.with_memory_space_constraint(x, pltpu.HBM) if places.get(k) is pltpu.HBM else x
        for k, x in enumerate(ins)
    ]
    in_specs = [pl.BlockSpec(memory_space=places.get(k, pltpu.VMEM)) for k in range(len(ins))]
    return pl.pallas_call(
        kernel,
        out_shape=[jax.ShapeDtypeStruct(shape, kind) for shape, kind in outs],
        in_specs=in_specs,
        out_specs=[pl.BlockSpec(memory_space=pltpu.VMEM)] * len(outs),
        scratch_shapes=list(scratch),
        compiler_params=pltpu.CompilerParams(vmem_limit_bytes=VMEM_LIMIT),
        cost_estimate=pl.CostEstimate(flops=flops, bytes_accessed=0, transcendentals=0),
    )(*ins)


def shifted(block, axis, distance):
    devices = range(lax.axis_size(axis))
    route = [(i - distance, i) for i in devices if i - distance in devices]
    return lax.ppermute(block, axis, route)


def exchange(up, down):
    return shifted(up, SFC, 1), shifted(down, SFC, -1)


def sum_over(rows, axes):
    return lax.all_to_all(rows, axes, 0, 0, tiled=True)


def body(
    right_side,
    cell_level,
    own_slot,
    near_slot,
    face_kind,
    orientation,
    penalty,
    send_slots,
    subface_maps,
):
    field_shape, planes_shape, index_shape = ((128, 128), f32), ((256, 128), f32), ((16, 128), jnp.int32)
    table_shape = ((640, 128), f32)
    messages = [((168, 128), f32)] * 2
    core = lax.axis_index("grp").astype(jnp.int32).reshape(1)
    tables = [jnp.asarray(table) for table in volume_tables()]
    row = ((1, 384), jnp.int32)
    (raw,) = call(
        pack_kernel,
        [((152, 128), f32)],
        [right_side, cell_level, own_slot, near_slot, face_kind, orientation, penalty, send_slots],
        [pltpu.VMEM(right_side.shape, f32), pltpu.VMEM((1, 128), jnp.int32)]
        + [pltpu.VMEM(*row)] * 4
        + [pltpu.VMEM((1, 384), f32), pltpu.VMEM(*row), pltpu.SemaphoreType.DMA((8,))],
        {k: pltpu.HBM for k in range(8)},
    )
    other = lax.ppermute(raw, "grp", [(0, 1), (1, 0)])
    half_shapes = [field_shape, planes_shape, index_shape, ((8, 128), f32)]
    *halves, grads, mass, up, down = call(
        first_kernel,
        half_shapes * 2 + [((128, 128), f32)] * 2 + messages,
        [core, raw, other] + tables,
        [pltpu.SemaphoreType.DMA((2,))],
        {0: pltpu.SMEM, 3: pltpu.HBM, 4: pltpu.HBM},
    )
    power0, planes, index, scale = zip(halves[:4], halves[4:])
    scratch = [pltpu.VMEM((224, 128), f32)] * 2 + [pltpu.VMEM((256, 128), f32)]
    got = exchange(up, down)
    volume0, volume1, plain, turned = call(
        volume_kernel,
        [field_shape, field_shape, table_shape, table_shape],
        [*power0, *scale, grads, mass, jnp.transpose(subface_maps, (1, 0, 2))],
        [pltpu.VMEM((WIDTH, 4, WIDTH), f32), pltpu.SemaphoreType.DMA],
        {6: pltpu.HBM},
        flops=10**7,
    )
    volume = (volume0, volume1)
    *halves, up, down = call(
        second_kernel,
        [field_shape, planes_shape, ((24, 128), f32), ((5120, 128), f32)] * 2 + messages,
        [*got, plain, turned]
        + [a[half] for half in range(2) for a in (planes, volume, index)],
        scratch,
    )
    power1, planes, meta, maps = zip(halves[:4], halves[4:])

    def middle(field, planes):
        volume0, sent0, volume1, sent1 = call(
            middle_kernel,
            [field_shape, planes_shape] * 2,
            [grads, mass]
            + [a[half] for half in range(2) for a in (field, scale, maps, planes, meta)],
            flops=10**7,
        )
        return (volume0, volume1), (sent0, sent1)

    got = exchange(up, down)
    volume, sent = middle(power1, planes)
    *halves, up, down = call(
        third_kernel,
        [field_shape, planes_shape] * 2 + messages,
        [*got] + [a[half] for half in range(2) for a in (planes, sent, volume, index, meta, maps)],
        scratch,
    )
    power2, planes = zip(halves[:2], halves[2:])
    got = exchange(up, down)
    volume, sent = middle(power2, planes)
    *power3, rows = call(
        fourth_kernel,
        [field_shape, field_shape, ((lax.axis_size(Z_AXIS), 128), f32)],
        [*got]
        + [a[half] for half in range(2) for a in (planes, sent, volume, index, meta, maps)]
        + [a[half] for half in range(2) for a in (power0, power1, power2)],
        scratch,
    )
    rows = sum_over(rows, Z_AXIS)
    (rows,) = call(repeat_sum_kernel, [((lax.axis_size(OTHERS), 128), f32)], [rows])
    rows = sum_over(rows, OTHERS)
    shape = (right_side.shape, f32)
    return tuple(
        call(
            last_kernel,
            [shape, shape],
            [core, rows]
            + [a[half] for half in range(2) for a in (power0, power1, power2, power3)],
            (),
            {0: pltpu.SMEM},
        )
    )


def solution(mesh):
    chips, cores = mesh.shape["sfc"], mesh.shape["grp"]
    sizes = (4, 4, chips // 16) if chips % 16 == 0 else (1, 1, chips)
    finer = Mesh(mesh.devices.reshape(*sizes, cores), SFC_GRP)
    split_cells = P(SFC_GRP)
    in_specs = (P(None, None, None, SFC_GRP),) + (split_cells,) * 7 + (P(),)
    out_specs = (P(None, None, None, SFC_GRP), P(None, None, None, SFC_GRP))
    return jax.shard_map(body, mesh=finer, in_specs=in_specs, out_specs=out_specs, check_vma=False)
```

```python
import functools

import jax
import jax.numpy as jnp
import numpy as np
from jax import lax
from jax.experimental import pallas as pl
from jax.experimental.pallas import tpu as pltpu
from jax.sharding import Mesh
from jax.sharding import PartitionSpec as P

NODES = 5
WIDTH = 25
CELLS = 128
GHOST = 96
ITERS = 3
SIGMA = 32.0
MASS_SHIFT = 1.0
Z_AXIS = ("sfc_2",)
OTHERS = ("sfc_0", "sfc_1")
SFC = ("sfc_0", "sfc_1", "sfc_2")
SFC_GRP = ("sfc_0", "sfc_1", "sfc_2", "grp")
VMEM_LIMIT = 24 * 1024 * 1024

f32 = jnp.float32
bf16 = jnp.bfloat16
highest = lax.Precision.HIGHEST


def node_tables():
    points = np.array([-1.0, -np.sqrt(3.0 / 7.0), 0.0, np.sqrt(3.0 / 7.0), 1.0])
    weights = np.array([0.1, 49.0 / 90.0, 32.0 / 45.0, 49.0 / 90.0, 0.1])
    identity = np.eye(5)
    spacing = points[:, None] - points[None, :] + identity
    barycentric = 1.0 / np.prod(spacing, axis=1)
    offdiag = barycentric[None, :] / barycentric[:, None] / spacing
    diagonal = np.sum(1.0 / spacing, axis=1) - 1.0
    derivs = np.where(identity > 0.5, diagonal[:, None], offdiag)
    stiffness = derivs.T @ (weights[:, None] * derivs)
    return stiffness, weights


STIFFNESS, WEIGHTS = node_tables()
FACE_MASS = [float(WEIGHTS[t // 5] * WEIGHTS[t % 5]) for t in range(WIDTH)]


def volume_tables():
    mass = np.diag(WEIGHTS)
    grads = (
        np.kron(np.kron(STIFFNESS, mass), mass)
        + np.kron(np.kron(mass, STIFFNESS), mass)
        + np.kron(np.kron(mass, mass), STIFFNESS)
    )
    full = np.zeros((128, 128), np.float32)
    full[:125, :125] = grads
    column = np.zeros((128, 128), np.float32)
    column[:125] = np.diag(np.kron(np.kron(mass, mass), mass))[:, None] * MASS_SHIFT
    return full, column


def face_node(face, t):
    high, low = t // 5, t % 5
    side = 4 * (face % 2)
    if face < 2:
        return 25 * side + t
    if face < 4:
        return 25 * high + 5 * side + low
    return 25 * high + 5 * low + side


def split(value):
    first = value.astype(bf16).astype(f32)
    rest = value - first
    second = rest.astype(bf16).astype(f32)
    third = (rest - second).astype(bf16).astype(f32)
    return first, second, third


def rev_first(planes, mask):
    return [jnp.where(mask, planes[5 * (4 - t // 5) + t % 5], planes[t]) for t in range(WIDTH)]


def rev_second(planes, mask):
    return [jnp.where(mask, planes[5 * (t // 5) + 4 - t % 5], planes[t]) for t in range(WIDTH)]


def swap(planes, mask):
    return [jnp.where(mask, planes[5 * (t % 5) + t // 5], planes[t]) for t in range(WIDTH)]


def orient_masks(codes):
    codes = codes.astype(jnp.int32)
    return (codes & 1) == 1, (codes & 2) == 2, (codes & 4) == 4


def orient_forward(planes, masks):
    return swap(rev_second(rev_first(planes, masks[0]), masks[1]), masks[2])


def orient_back(planes, masks):
    return rev_first(rev_second(swap(planes, masks[2]), masks[1]), masks[0])


def read_planes(ref, count=WIDTH):
    return [ref[8 * t : 8 * t + 8, :] for t in range(count)]


def gather_planes(field, face, cell):
    rows = {}

    def at(node):
        if node not in rows:
            row = jnp.broadcast_to(field[node : node + 1, :], (8, 128))
            rows[node] = jnp.take_along_axis(row, cell, axis=1, mode="promise_in_bounds")
        return rows[node]

    masks = [face == k for k in range(5)]
    planes = []
    for t in range(WIDTH):
        value = at(face_node(5, t))
        for k in range(5):
            value = jnp.where(masks[k], at(face_node(k, t)), value)
        planes.append(value)
    return planes


def write_messages(even, sources, first_ref, second_ref):
    @pl.when(even)
    def _():
        fill_messages(sources, first_ref, second_ref)

    @pl.when(jnp.logical_not(even))
    def _():
        fill_messages(sources, second_ref, first_ref)


def fill_messages(sources, up_ref, down_ref):

    def pair(ref, start, source, sent, own):
        ref[pl.ds(start, 28, stride=2), :] = source[pl.ds(4 + sent, 28, stride=8), :]
        ref[pl.ds(start + 1, 28, stride=2), :] = source[pl.ds(own, 28, stride=8), :]

    for half in range(2):
        pair(up_ref, 56 * half, sources[half], 2, 3)
        pair(down_ref, 56 * half, sources[half], 3, 2)
    pair(up_ref, 112, sources[1], 0, 1)
    pair(down_ref, 112, sources[0], 1, 0)


def pack_kernel(
    rhs_hbm,
    level_hbm,
    own_hbm,
    near_hbm,
    kind_hbm,
    orient_hbm,
    penalty_hbm,
    send_hbm,
    raw_ref,
    rhs_ref,
    level_ref,
    own_ref,
    near_ref,
    kind_ref,
    orient_ref,
    penalty_ref,
    send_ref,
    sems,
):
    copies = [
        pltpu.make_async_copy(source, target, sems.at[k])
        for k, (source, target) in enumerate(
            (
                (own_hbm, own_ref.at[0]),
                (near_hbm, near_ref.at[0]),
                (kind_hbm, kind_ref.at[0]),
                (orient_hbm, orient_ref.at[0]),
                (penalty_hbm, penalty_ref.at[0]),
                (send_hbm, send_ref.at[0]),
                (level_hbm, level_ref.at[0]),
                (rhs_hbm, rhs_ref),
            )
        )
    ]
    for copy in copies:
        copy.start()
    for copy in copies:
        copy.wait()
    for a in range(5):
        for b in range(5):
            raw_ref[25 * a + 5 * b : 25 * a + 5 * b + 5, :] = rhs_ref[a, b]
    raw_ref[125:128, :] = jnp.zeros((3, 128), f32)
    for k, ref in enumerate((own_ref, near_ref, kind_ref, orient_ref, penalty_ref, send_ref)):
        for third in range(3):
            at = 128 + 3 * k + third
            raw_ref[at : at + 1, :] = ref[:, 128 * third : 128 * third + 128].astype(f32)
    raw_ref[146:147, :] = level_ref[...].astype(f32)
    raw_ref[147:152, :] = jnp.zeros((5, 128), f32)


def first_kernel(place_ref, mine_ref, other_ref, grads_hbm, mass_hbm, *refs):
    outs, (grads_ref, mass_ref, up_ref, down_ref, sems) = refs[:8], refs[8:]
    even = place_ref[1] == 0
    copies = [
        pltpu.make_async_copy(grads_hbm, grads_ref, sems.at[0]),
        pltpu.make_async_copy(mass_hbm, mass_ref, sems.at[1]),
    ]
    for copy in copies:
        copy.start()
    low = place_ref[0] == 0
    for half in range(2):
        first, second = (mine_ref, other_ref) if half == 0 else (other_ref, mine_ref)
        outs[4 * half][...] = jnp.where(low, first[0:128, :], second[0:128, :])
        raw = jnp.where(low, first[128:152, :], second[128:152, :])
        prepare_half(raw, *outs[4 * half : 4 * half + 4])
    write_messages(even, (outs[1], outs[5]), up_ref, down_ref)
    for copy in copies:
        copy.wait()


def prepare_half(raw, field_ref, planes_ref, index_ref, scale_ref):
    def entries(k):
        return jnp.concatenate([raw[3 * k + third : 3 * k + third + 1] for third in range(3)], axis=1)

    own = entries(0).astype(jnp.int32)
    near = entries(1).astype(jnp.int32)
    pieces = split(entries(4))
    rows = [
        (own >> 7).astype(f32),
        (own & 127).astype(f32),
        entries(2),
        entries(3),
        pieces[0],
        pieces[1],
        pieces[2],
        jnp.zeros((1, 384), f32),
    ]
    table = jnp.concatenate(rows, axis=0).astype(bf16)
    spot = lax.broadcasted_iota(jnp.int32, (512, 384), 0)
    lane = spot & 127
    wanted = jnp.where(lane < GHOST, 6 * CELLS + (spot >> 7) * GHOST + lane, -1)
    onehot = jnp.where(wanted == near, 1.0, 0.0).astype(bf16)
    moved = lax.dot_general(
        table, onehot, (((1,), (1,)), ((), ())), preferred_element_type=f32
    )
    zeros = jnp.zeros((4, 128), f32)

    def upper(row):
        parts = [row[:, 128 * k : 128 * k + 128] for k in range(4)]
        return jnp.concatenate(parts + [zeros], axis=0)

    own_face, own_cell = upper(moved[0:1]), upper(moved[1:2])
    penalty = upper(moved[4:5] + moved[5:6] + moved[6:7])
    lanes = lax.broadcasted_iota(jnp.int32, (1, 128), 1)
    sends = entries(5).astype(jnp.int32)
    send = [
        jnp.where(lanes < GHOST, pltpu.roll(sends, (384 - GHOST * k) % 384, 1)[:, :128], 0)
        for k in range(4)
    ]
    send = jnp.concatenate([jnp.zeros((4, 128), jnp.int32)] + send, axis=0)
    sub = lax.broadcasted_iota(jnp.int32, (8, 128), 0)
    face = jnp.where(sub < 4, own_face.astype(jnp.int32), send >> 7)
    cell = jnp.where(sub < 4, own_cell.astype(jnp.int32), send & 127)
    index_ref[0:8, :] = face
    index_ref[8:16, :] = cell
    scale = jnp.exp2(-jnp.broadcast_to(raw[18:19], (8, 128)))
    scale_ref[...] = scale
    scaled = penalty * jnp.take_along_axis(scale, cell, axis=1, mode="promise_in_bounds")
    for t, plane in enumerate(gather_planes(field_ref, face, cell)):
        planes_ref[8 * t : 8 * t + 8, :] = plane
    planes_ref[200:208, :] = upper(moved[2:3])
    planes_ref[208:216, :] = upper(moved[3:4])
    planes_ref[216:224, :] = scaled


def local_volume(field, scale_ref, grads_ref, mass_ref):
    scale = scale_ref[0:1, :]
    grads = jnp.dot(grads_ref[...], field, precision=highest, preferred_element_type=f32)
    return scale * grads + (scale * scale * scale) * (mass_ref[...] * field)


def volume_kernel(
    field0_ref,
    field1_ref,
    scale0_ref,
    scale1_ref,
    grads_ref,
    mass_ref,
    subface_hbm,
    volume0_ref,
    volume1_ref,
    plain_ref,
    turned_ref,
    subface_ref,
    sem,
):
    copy = pltpu.make_async_copy(subface_hbm, subface_ref, sem)
    copy.start()
    volume0_ref[...] = local_volume(field0_ref[...], scale0_ref, grads_ref, mass_ref)
    volume1_ref[...] = local_volume(field1_ref[...], scale1_ref, grads_ref, mass_ref)
    plain_ref[...] = jnp.zeros((640, 128), f32)
    turned_ref[...] = jnp.zeros((640, 128), f32)
    copy.wait()
    lane = lax.broadcasted_iota(jnp.int32, (4, WIDTH), 1)
    sub = lax.broadcasted_iota(jnp.int32, (4, WIDTH), 0)
    for i in range(WIDTH):
        unit = jnp.where((lane == i) & (sub == 0), 1.0, 0.0)
        rows = jnp.concatenate([subface_ref[i], unit], axis=0)
        rows = jnp.concatenate(split(rows), axis=0)
        columns = jnp.transpose(rows)
        plain_ref[25 * i : 25 * i + 25, 0:24] = columns
        turned_ref[pl.ds(i, 25, stride=25), 0:24] = columns


def map_sent(maps_ref, planes_ref, meta_ref, masks):
    turned = orient_forward(read_planes(planes_ref), masks)
    result = []
    for i in range(WIDTH):
        total = None
        for j in range(WIDTH):
            at = 8 * (WIDTH * j + i)
            term = maps_ref[at : at + 8, :] * turned[j]
            total = term if total is None else total + term
        result.append(total)
    return result


def middle_kernel(grads_ref, mass_ref, *refs):
    for half in range(2):
        field_ref, scale_ref, maps_ref, planes_ref, meta_ref = refs[5 * half : 5 * half + 5]
        volume_ref, sent_ref = refs[10 + 2 * half : 12 + 2 * half]
        volume_ref[...] = local_volume(field_ref[...], scale_ref, grads_ref, mass_ref)
        masks = orient_masks(meta_ref[8:16, :])
        for t, plane in enumerate(map_sent(maps_ref, planes_ref, meta_ref, masks)):
            sent_ref[8 * t : 8 * t + 8, :] = plane


def read_messages(even, first_ref, second_ref, sources, gots):
    def put(half, row, value):
        gots[half][pl.ds(row, 28, stride=8), :] = value

    def rows(when_even_ref, when_odd_ref, start):
        at = pl.ds(start, 28, stride=2)
        return jnp.where(even, when_even_ref[at, :], when_odd_ref[at, :])

    def below(start):
        return rows(second_ref, first_ref, start)

    def above(start):
        return rows(first_ref, second_ref, start)

    def local(half, row):
        return sources[half][pl.ds(row, 28, stride=8), :]

    for half in range(2):
        put(half, 2, below(56 * half))
        put(half, 7, below(56 * half + 1))
        put(half, 3, above(56 * half))
        put(half, 6, above(56 * half + 1))
    put(0, 0, below(112))
    put(0, 5, below(113))
    put(1, 1, above(112))
    put(1, 4, above(113))
    put(0, 1, local(1, 5))
    put(0, 4, local(1, 0))
    put(1, 0, local(0, 4))
    put(1, 5, local(0, 1))


def build_maps(plain_ref, turned_ref, kind, maps_ref):
    code = lax.broadcasted_iota(jnp.int32, (8, 128), 0)
    code = jnp.where(code < 4, code + 2, jnp.where(code == 4, 1, -1)).astype(f32)
    for half, table_ref in enumerate((plain_ref, turned_ref)):
        table = table_ref[...].astype(bf16)
        chosen = []
        for row in range(4 * half, 4 * half + 4):
            chosen.append(jnp.where(code == kind[row : row + 1, :], 1.0, 0.0))
        chosen = jnp.concatenate(chosen, axis=1)
        unused = jnp.zeros((104, 512), f32)
        chosen = jnp.concatenate([chosen] * 3 + [unused], axis=0).astype(bf16)
        values = jnp.dot(table, chosen, preferred_element_type=f32)
        for k in range(4):
            maps_ref[pl.ds(4 * half + k, 640, stride=8), :] = values[:, 128 * k : 128 * k + 128]


def add_faces(volume_ref, planes, index_ref, pieces_ref, field_ref):
    for t, plane in enumerate(planes):
        pieces_ref[8 * t : 8 * t + 8, :] = plane
    pieces_ref[200:256, :] = jnp.zeros((56, 128), f32)
    face, cell = index_ref[0:8, :], index_ref[8:16, :]
    key = (face & 1) * 128 + cell
    axis = face >> 1
    slot = lax.broadcasted_iota(jnp.int32, (256, 128), 0)
    left, right = [], []
    for row in range(8):
        value = jnp.concatenate(split(pieces_ref[pl.ds(row, 32, stride=8), :]), axis=0)
        chosen = axis[row : row + 1, :]
        left.append(
            jnp.concatenate([jnp.where(chosen == k, value, 0.0) for k in range(3)], axis=0).astype(
                bf16
            )
        )
        right.append(jnp.where(slot == key[row : row + 1, :], 1.0, 0.0).astype(bf16))
    total = lax.dot_general(
        jnp.concatenate(left, axis=1),
        jnp.concatenate(right, axis=1),
        (((1,), (1,)), ((), ())),
        preferred_element_type=f32,
    )
    total = total * (1.0 / SIGMA)
    field_ref[...] = volume_ref[...] * (1.0 / SIGMA)
    for k in range(3):
        part = total[96 * k : 96 * k + 32] + total[96 * k + 32 : 96 * k + 64]
        part = part + total[96 * k + 64 : 96 * k + 96]
        for side in range(2):
            value = part[:WIDTH, 128 * side : 128 * side + 128]
            if k == 0:
                field_ref[100 * side : 100 * side + 25, :] += value
            elif k == 1:
                for a in range(5):
                    at = 25 * a + 20 * side
                    field_ref[at : at + 5, :] += value[5 * a : 5 * a + 5]
            else:
                field_ref[pl.ds(4 * side, 25, stride=5), :] += value


def combine(got_ref, planes_ref, sent, maps_ref, penalty, masks):
    sub = lax.broadcasted_iota(jnp.int32, (8, 128), 0)
    owned = sub < 4
    got = read_planes(got_ref)
    turned = orient_forward(got, masks)
    mixed = [
        jnp.where(owned, turned[t], (penalty * FACE_MASS[t]) * (got[t] - sent[t]))
        for t in range(WIDTH)
    ]
    mapped = []
    for i in range(WIDTH):
        total = None
        for j in range(WIDTH):
            at = 8 * (WIDTH * i + j)
            term = maps_ref[at : at + 8, :] * mixed[j]
            total = term if total is None else total + term
        mapped.append(total)
    back = orient_back(mapped, masks)
    return [
        jnp.where(
            owned,
            (penalty * FACE_MASS[t]) * (planes_ref[8 * t : 8 * t + 8, :] - mapped[t]),
            -back[t],
        )
        for t in range(WIDTH)
    ]


def next_planes(field_ref, index_ref, planes_ref):
    face, cell = index_ref[0:8, :], index_ref[8:16, :]
    for t, plane in enumerate(gather_planes(field_ref, face, cell)):
        planes_ref[8 * t : 8 * t + 8, :] = plane
    planes_ref[200:224, :] = jnp.zeros((24, 128), f32)


def second_kernel(place_ref, came_first_ref, came_second_ref, plain_ref, turned_ref, *refs):
    ins, outs = (refs[0:3], refs[3:6]), (refs[6:10], refs[10:14])
    up_ref, down_ref, got0_ref, got1_ref, pieces_ref = refs[14:]
    gots = (got0_ref, got1_ref)
    even = place_ref[1] == 0
    read_messages(even, came_first_ref, came_second_ref, (ins[0][0], ins[1][0]), gots)
    sub = lax.broadcasted_iota(jnp.int32, (8, 128), 0)
    for half in range(2):
        old_ref, volume_ref, index_ref = ins[half]
        field_ref, planes_ref, meta_ref, maps_ref = outs[half]
        got_ref = gots[half]
        for k in range(3):
            at = 200 + 8 * k
            meta_ref[8 * k : 8 * k + 8, :] = jnp.where(
                sub < 4, old_ref[at : at + 8, :], got_ref[at : at + 8, :]
            )
        masks = orient_masks(meta_ref[8:16, :])
        build_maps(plain_ref, turned_ref, meta_ref[0:8, :], maps_ref)
        sent = map_sent(maps_ref, old_ref, meta_ref, masks)
        planes = combine(got_ref, old_ref, sent, maps_ref, meta_ref[16:24, :], masks)
        add_faces(volume_ref, planes, index_ref, pieces_ref, field_ref)
        next_planes(field_ref, index_ref, planes_ref)
    write_messages(even, (outs[0][1], outs[1][1]), up_ref, down_ref)


def apply_half(got_ref, ins, pieces_ref, field_ref):
    old_ref, sent_ref, volume_ref, index_ref, meta_ref, maps_ref = ins
    masks = orient_masks(meta_ref[8:16, :])
    sent = read_planes(sent_ref)
    planes = combine(got_ref, old_ref, sent, maps_ref, meta_ref[16:24, :], masks)
    add_faces(volume_ref, planes, index_ref, pieces_ref, field_ref)


def third_kernel(place_ref, came_first_ref, came_second_ref, *refs):
    ins, outs = (refs[0:6], refs[6:12]), (refs[12:14], refs[14:16])
    up_ref, down_ref, got0_ref, got1_ref, pieces_ref = refs[16:]
    gots = (got0_ref, got1_ref)
    even = place_ref[1] == 0
    read_messages(even, came_first_ref, came_second_ref, (ins[0][0], ins[1][0]), gots)
    for half in range(2):
        field_ref, planes_ref = outs[half]
        apply_half(gots[half], ins[half], pieces_ref, field_ref)
        next_planes(field_ref, ins[half][3], planes_ref)
    write_messages(even, (outs[0][1], outs[1][1]), up_ref, down_ref)


def fourth_kernel(place_ref, came_first_ref, came_second_ref, *refs):
    ins, old_powers = (refs[0:6], refs[6:12]), (refs[12:15], refs[15:18])
    fields, (moments_ref, got0_ref, got1_ref, pieces_ref) = refs[18:20], refs[20:]
    gots = (got0_ref, got1_ref)
    even = place_ref[1] == 0
    read_messages(even, came_first_ref, came_second_ref, (ins[0][0], ins[1][0]), gots)
    for half in range(2):
        apply_half(gots[half], ins[half], pieces_ref, fields[half])
    powers = [
        [ref[...] for ref in old_powers[half]] + [fields[half][...]] for half in range(2)
    ]
    lane = lax.broadcasted_iota(jnp.int32, (1, 128), 1)
    result = jnp.zeros((1, 128), f32)
    for k in range(2 * ITERS):
        both = sum(powers[half][k // 2] * powers[half][(k + 1) // 2] for half in range(2))
        row = jnp.sum(both, axis=0, keepdims=True)
        result = jnp.where(lane == k, jnp.sum(row, axis=1, keepdims=True), result)
    moments_ref[...] = jnp.broadcast_to(result, moments_ref.shape)


def repeat_sum_kernel(rows_ref, out_ref):
    total = jnp.sum(rows_ref[...], axis=0, keepdims=True)
    out_ref[...] = jnp.broadcast_to(total, out_ref.shape)


def coefficients(moments):
    def inner(one, two, shift):
        total = None
        for i in range(len(one)):
            for j in range(len(two)):
                term = one[i] * two[j] * moments[i + j + shift]
                total = term if total is None else total + term
        return total

    unit = jnp.ones_like(moments[0])
    none = jnp.zeros_like(moments[0])
    iterate, remains, search = [], [unit], [unit]
    norm_now = moments[0]
    for iteration in range(ITERS):
        step = norm_now / inner(search, search, 1)
        iterate = [
            (iterate[i] if i < len(iterate) else none) + step * search[i]
            for i in range(len(search))
        ]
        image = [none] + search
        remains = [
            (remains[i] if i < len(remains) else none) - step * image[i]
            for i in range(len(image))
        ]
        if iteration + 1 < ITERS:
            norm_next = inner(remains, remains, 0)
            blend = norm_next / norm_now
            search = [
                remains[i] + (blend * search[i] if i < len(search) else none)
                for i in range(len(remains))
            ]
            norm_now = norm_next
    return iterate, remains


def last_kernel(place_ref, rows_ref, *refs):
    halves, (solution_ref, residual_ref) = (refs[0:4], refs[4:8]), refs[8:]
    low = place_ref[0] == 0
    total = jnp.sum(rows_ref[...], axis=0, keepdims=True)
    lane = lax.broadcasted_iota(jnp.int32, (1, 128), 1)
    moments = [
        jnp.broadcast_to(
            jnp.sum(jnp.where(lane == k, total, 0.0), axis=1, keepdims=True), (1, 128)
        )
        for k in range(2 * ITERS)
    ]
    iterate, remains = coefficients(moments)
    for a in range(5):
        for b in range(5):
            at = 25 * a + 5 * b
            values = [
                jnp.where(low, one[at : at + 5, :], two[at : at + 5, :]) for one, two in zip(*halves)
            ]
            answer = sum((c * (1.0 / SIGMA)) * v for c, v in zip(iterate, values))
            solution_ref[a, b] = answer
            residual_ref[a, b] = sum(c * v for c, v in zip(remains, values))


def call(kernel, outs, ins, scratch=(), places=None, flops=0):
    places = places or {}
    ins = [
        pltpu.with_memory_space_constraint(x, pltpu.HBM) if places.get(k) is pltpu.HBM else x
        for k, x in enumerate(ins)
    ]
    in_specs = [pl.BlockSpec(memory_space=places.get(k, pltpu.VMEM)) for k in range(len(ins))]
    return pl.pallas_call(
        kernel,
        out_shape=[jax.ShapeDtypeStruct(shape, kind) for shape, kind in outs],
        in_specs=in_specs,
        out_specs=[pl.BlockSpec(memory_space=pltpu.VMEM)] * len(outs),
        scratch_shapes=list(scratch),
        compiler_params=pltpu.CompilerParams(vmem_limit_bytes=VMEM_LIMIT),
        cost_estimate=pl.CostEstimate(flops=flops, bytes_accessed=0, transcendentals=0),
    )(*ins)


def paired(block, start):
    chips = lax.axis_size(SFC)
    lower = range(start, chips - 1, 2)
    return lax.ppermute(block, SFC, [(i, i + 1) for i in lower] + [(i + 1, i) for i in lower])


def exchange(first, second):
    return paired(first, 0), paired(second, 1)


def sum_over(rows, axes):
    return lax.all_to_all(rows, axes, 0, 0, tiled=True)


def body(
    right_side,
    cell_level,
    own_slot,
    near_slot,
    face_kind,
    orientation,
    penalty,
    send_slots,
    subface_maps,
):
    field_shape, planes_shape, index_shape = ((128, 128), f32), ((256, 128), f32), ((16, 128), jnp.int32)
    table_shape = ((640, 128), f32)
    messages = [((168, 128), f32)] * 2
    place = jnp.stack([lax.axis_index("grp"), lax.axis_index("sfc_2") & 1]).astype(jnp.int32)
    tables = [jnp.asarray(table) for table in volume_tables()]
    row = ((1, 384), jnp.int32)
    (raw,) = call(
        pack_kernel,
        [((152, 128), f32)],
        [right_side, cell_level, own_slot, near_slot, face_kind, orientation, penalty, send_slots],
        [pltpu.VMEM(right_side.shape, f32), pltpu.VMEM((1, 128), jnp.int32)]
        + [pltpu.VMEM(*row)] * 4
        + [pltpu.VMEM((1, 384), f32), pltpu.VMEM(*row), pltpu.SemaphoreType.DMA((8,))],
        {k: pltpu.HBM for k in range(8)},
    )
    other = lax.ppermute(raw, "grp", [(0, 1), (1, 0)])
    half_shapes = [field_shape, planes_shape, index_shape, ((8, 128), f32)]
    *halves, grads, mass, up, down = call(
        first_kernel,
        half_shapes * 2 + [((128, 128), f32)] * 2 + messages,
        [place, raw, other] + tables,
        [pltpu.SemaphoreType.DMA((2,))],
        {0: pltpu.SMEM, 3: pltpu.HBM, 4: pltpu.HBM},
    )
    power0, planes, index, scale = zip(halves[:4], halves[4:])
    scratch = [pltpu.VMEM((224, 128), f32)] * 2 + [pltpu.VMEM((256, 128), f32)]
    got = exchange(up, down)
    volume0, volume1, plain, turned = call(
        volume_kernel,
        [field_shape, field_shape, table_shape, table_shape],
        [*power0, *scale, grads, mass, jnp.transpose(subface_maps, (1, 0, 2))],
        [pltpu.VMEM((WIDTH, 4, WIDTH), f32), pltpu.SemaphoreType.DMA],
        {6: pltpu.HBM},
        flops=10**7,
    )
    volume = (volume0, volume1)
    *halves, up, down = call(
        second_kernel,
        [field_shape, planes_shape, ((24, 128), f32), ((5120, 128), f32)] * 2 + messages,
        [place, *got, plain, turned]
        + [a[half] for half in range(2) for a in (planes, volume, index)],
        scratch,
        {0: pltpu.SMEM},
    )
    power1, planes, meta, maps = zip(halves[:4], halves[4:])

    def middle(field, planes):
        volume0, sent0, volume1, sent1 = call(
            middle_kernel,
            [field_shape, planes_shape] * 2,
            [grads, mass]
            + [a[half] for half in range(2) for a in (field, scale, maps, planes, meta)],
            flops=10**7,
        )
        return (volume0, volume1), (sent0, sent1)

    got = exchange(up, down)
    volume, sent = middle(power1, planes)
    *halves, up, down = call(
        third_kernel,
        [field_shape, planes_shape] * 2 + messages,
        [place, *got]
        + [a[half] for half in range(2) for a in (planes, sent, volume, index, meta, maps)],
        scratch,
        {0: pltpu.SMEM},
    )
    power2, planes = zip(halves[:2], halves[2:])
    got = exchange(up, down)
    volume, sent = middle(power2, planes)
    *power3, rows = call(
        fourth_kernel,
        [field_shape, field_shape, ((lax.axis_size(Z_AXIS), 128), f32)],
        [place, *got]
        + [a[half] for half in range(2) for a in (planes, sent, volume, index, meta, maps)]
        + [a[half] for half in range(2) for a in (power0, power1, power2)],
        scratch,
        {0: pltpu.SMEM},
    )
    rows = sum_over(rows, Z_AXIS)
    (rows,) = call(repeat_sum_kernel, [((lax.axis_size(OTHERS), 128), f32)], [rows])
    rows = sum_over(rows, OTHERS)
    shape = (right_side.shape, f32)
    return tuple(
        call(
            last_kernel,
            [shape, shape],
            [place, rows]
            + [a[half] for half in range(2) for a in (power0, power1, power2, power3)],
            (),
            {0: pltpu.SMEM},
        )
    )


def solution(mesh):
    chips, cores = mesh.shape["sfc"], mesh.shape["grp"]
    sizes = (4, 4, chips // 16) if chips % 16 == 0 else (1, 1, chips)
    finer = Mesh(mesh.devices.reshape(*sizes, cores), SFC_GRP)
    split_cells = P(SFC_GRP)
    in_specs = (P(None, None, None, SFC_GRP),) + (split_cells,) * 7 + (P(),)
    out_specs = (P(None, None, None, SFC_GRP), P(None, None, None, SFC_GRP))
    return jax.shard_map(body, mesh=finer, in_specs=in_specs, out_specs=out_specs, check_vma=False)
```
